32 devices in a mesh: bead: 4 (over y, x), dom: 8 (over z, core).
Axes of the slice: x: 2, y: 2, z: 4, core: 2. Of those that a mesh axis runs over, the one named last changes fastest.
Arguments:
- mode_pos: float32 [16, 3, 6144], P('bead', None, 'dom'), may hold values from -6 to 6
- mode_vel: float32 [16, 3, 6144], P('bead', None, 'dom'), may hold values from -6 to 6
- charges: float32 [6144], P('dom'), may hold values from -1.5 to 1.5
Outputs:
- positions: float32 [16, 3, 6144], P('bead', None, 'dom')
- velocities: float32 [16, 3, 6144], P('bead', None, 'dom')
The draws below stay inside these ranges and needn't reach their ends.
All inputs are finite; a program needn't handle non-finite values.
Results may differ from the reference program's by a relative error of at most 0.0003.
Values sent between devices are 32-bit elements; how exact they have to be, the bound alone decides.
A program may use at most 64 MiB of HBM per device.

```python
import jax
import jax.numpy as jnp
from jax import lax

BEADS = 16
PART_DEV = 768
PARTICLES = 6144
N_DOM = 8


def level_of(own_key, shape, shards, least, top_value):
    def one(dim, shards_of):
        draws = jax.random.uniform(jax.random.fold_in(jax.random.fold_in(own_key, 6), dim), (shards_of,), jnp.float32, least / len(shards), top_value / len(shards))
        return jnp.repeat(jnp.exp(draws), shape[dim] // shards_of).reshape((-1,) + (1,) * (len(shape) - dim - 1))

    loudness = one(*shards[0])
    for cut in shards[1:]:
        loudness = loudness * one(*cut)
    return loudness


def scatter_about(own_key, extent, spread, reach, split=(), kind=jnp.bfloat16):
    factor_of = level_of(own_key, extent, split, -0.22, 0.18) if split else 1.0
    array = jax.random.normal(own_key, extent, jnp.float32) * spread * factor_of
    return jnp.minimum(jnp.maximum(array, -reach), reach).astype(kind)


def setup_inputs(seed: int = 0) -> dict:
    streams_of = jax.random.split(jax.random.key(seed), 4)
    mode_pos = scatter_about(streams_of[0], (BEADS, 3, PARTICLES), 1.0, 6.0, ((0, 4), (2, 8)), jnp.float32)
    mode_vel = scatter_about(streams_of[1], (BEADS, 3, PARTICLES), 1.0, 6.0, ((0, 4), (2, 8)), jnp.float32)
    charges = jnp.clip(jax.random.uniform(streams_of[2], (PARTICLES,), jnp.float32, -1.5, 1.5) * level_of(streams_of[2], (PARTICLES,), ((0, 8),), -0.4, 0.0), -1.5, 1.5)
    return dict(mode_pos=mode_pos, mode_vel=mode_vel, charges=charges)


KAPPA = 2.0
SOFTEN = 0.09
KICK = 0.3
OMEGA = 7.0
STEP_TIME = 0.1
HIGHEST = lax.Precision.HIGHEST

def mode_table(bead_index, mode_index):
    scale_root = jnp.sqrt(jnp.float32(BEADS))
    angle = 2.0 * jnp.pi * bead_index.astype(jnp.float32) * mode_index.astype(jnp.float32) / BEADS
    first = jnp.ones_like(angle) / scale_root
    middle = jnp.cos(jnp.pi * bead_index.astype(jnp.float32)) / scale_root + 0.0 * angle
    factor = jnp.sqrt(2.0 / jnp.float32(BEADS))
    return jnp.where(mode_index == 0, first, jnp.where(2 * mode_index < BEADS, factor * jnp.cos(angle), jnp.where(2 * mode_index == BEADS, middle, factor * jnp.sin(angle))))

def evolve(mode_pos, mode_vel, mode_index):
    freq = 2.0 * OMEGA * jnp.sin(jnp.pi * mode_index.astype(jnp.float32) / BEADS)
    theta = freq * STEP_TIME
    cosine = jnp.cos(theta)[:, None, None]
    sine = jnp.sin(theta)
    safe_freq = jnp.where(mode_index > 0, freq, 1.0)
    carry_rate = jnp.where(mode_index > 0, sine / safe_freq, STEP_TIME)[:, None, None]
    new_pos = cosine * mode_pos + carry_rate * mode_vel
    new_vel = (-freq * sine)[:, None, None] * mode_pos + cosine * mode_vel
    return (new_pos, new_vel)

def pair_force(near_pos, near_charge, far_pos, far_charge):
    delta = near_pos[:, :, :, None] - far_pos[:, :, None, :]
    square = lax.optimization_barrier(jnp.sum(delta * delta, axis=1)) + SOFTEN
    distance = jnp.sqrt(square)
    weight = near_charge[None, :, None] * far_charge[None, None, :] * jnp.exp(-KAPPA * distance) * (1.0 + KAPPA * distance) / (square * distance)
    return lax.optimization_barrier(jnp.sum(weight[:, None] * delta, axis=3))

def reference(mode_pos, mode_vel, charges):
    modes = jnp.arange(BEADS, dtype=jnp.int32)
    new_pos, new_vel = evolve(mode_pos, mode_vel, modes)
    table = mode_table(modes[:, None], modes[None, :])
    positions = jnp.einsum('bk,kcn->bcn', table, new_pos, precision=HIGHEST)
    bead_vel = jnp.einsum('bk,kcn->bcn', table, new_vel, precision=HIGHEST)

    def bead_force(bead_pos):
        whole = bead_pos[None]

        def one_block(block_index):
            start = (block_index * PART_DEV).astype(jnp.int32)
            near = lax.dynamic_slice_in_dim(whole, start, PART_DEV, 2)
            near_charge = lax.dynamic_slice_in_dim(charges, start, PART_DEV, 0)
            return pair_force(near, near_charge, whole, charges)[0]
        blocks = lax.map(one_block, jnp.arange(N_DOM, dtype=jnp.int32))
        return jnp.transpose(blocks, (1, 0, 2)).reshape(3, PARTICLES)
    forces = lax.map(bead_force, positions)
    return (positions, bead_vel + KICK * forces)
```

```python
import functools

import jax
import jax.numpy as jnp
from jax import lax
from jax.experimental import pallas as pl
from jax.experimental.pallas import tpu as pltpu
from jax.sharding import PartitionSpec as P

BEADS = 16


KAPPA = 2.0
SOFTEN = 0.09
KICK = 0.3
OMEGA = 7.0
STEP_TIME = 0.1
HIGHEST = lax.Precision.HIGHEST
LOG2E = 1.4426950408889634
ROWS = 256


def mode_table(bead_index, mode_index):
    scale_root = jnp.sqrt(jnp.float32(BEADS))
    angle = 2.0 * jnp.pi * bead_index.astype(jnp.float32) * mode_index.astype(jnp.float32) / BEADS
    first = jnp.ones_like(angle) / scale_root
    middle = jnp.cos(jnp.pi * bead_index.astype(jnp.float32)) / scale_root + 0.0 * angle
    factor = jnp.sqrt(2.0 / jnp.float32(BEADS))
    return jnp.where(
        mode_index == 0,
        first,
        jnp.where(
            2 * mode_index < BEADS,
            factor * jnp.cos(angle),
            jnp.where(2 * mode_index == BEADS, middle, factor * jnp.sin(angle)),
        ),
    )


def evolve(mode_pos, mode_vel, mode_index):
    freq = 2.0 * OMEGA * jnp.sin(jnp.pi * mode_index.astype(jnp.float32) / BEADS)
    theta = freq * STEP_TIME
    cosine = jnp.cos(theta)[:, None, None]
    sine = jnp.sin(theta)
    safe_freq = jnp.where(mode_index > 0, freq, 1.0)
    carry_rate = jnp.where(mode_index > 0, sine / safe_freq, STEP_TIME)[:, None, None]
    new_pos = cosine * mode_pos + carry_rate * mode_vel
    new_vel = (-freq * sine)[:, None, None] * mode_pos + cosine * mode_vel
    return (new_pos, new_vel)


def split3(value):
    one = value.astype(jnp.bfloat16).astype(jnp.float32)
    rest = value - one
    two = rest.astype(jnp.bfloat16).astype(jnp.float32)
    return one, two, rest - two


def row_index(shape):
    return lax.broadcasted_iota(jnp.int32, shape, 0)


def scaled(pack, centre):
    return jnp.where(row_index(pack.shape) < 3, KAPPA * (pack - centre), 0.0)


def near_operand(pos):
    row = row_index(pos.shape)
    norm = jnp.sum(pos * pos, axis=0, keepdims=True) + KAPPA * KAPPA * SOFTEN
    one, two, three = split3(jnp.where(row == 3, norm, -2.0 * pos))
    last = row == 3
    groups = (
        one,
        jnp.where(last, two, one),
        jnp.where(last, three, two),
        jnp.where(last, 1.0, two),
        jnp.where(last, 1.0, one),
        jnp.where(last, 1.0, three),
    )
    return jnp.concatenate(groups, axis=0).astype(jnp.bfloat16)


def far_operands(pos, charge):
    row = row_index(pos.shape)
    last = row == 3
    norm = jnp.sum(pos * pos, axis=0, keepdims=True)
    one, two, three = split3(jnp.where(last, norm, pos))
    first = jnp.where(last, 1.0, one)
    groups = (
        first,
        jnp.where(last, 1.0, two),
        first,
        jnp.where(last, one, two),
        jnp.where(last, two, three),
        jnp.where(last, three, one),
    )
    left = jnp.concatenate(groups, axis=0).T.astype(jnp.bfloat16)
    moments = jnp.where(last, charge, pos * charge)
    parts = split3(moments) + (jnp.zeros_like(pos),)
    right = jnp.concatenate(parts, axis=0).astype(jnp.bfloat16)
    return left, right


def pair_weight(square):
    inverse = lax.rsqrt(square)
    decay = jnp.exp2(square * (inverse * (-LOG2E)))
    return decay * (1.0 + inverse) * (inverse * inverse)


def force_sums(left, right, near):
    total = None
    for start in range(0, left.shape[0], ROWS):
        square = jnp.dot(left[start : start + ROWS], near, preferred_element_type=jnp.float32)
        weight = pair_weight(square)
        high = weight.astype(jnp.bfloat16)
        low = (weight - high.astype(jnp.float32)).astype(jnp.bfloat16)
        moment = right[:, start : start + ROWS]
        part = jnp.dot(moment, high, preferred_element_type=jnp.float32)
        part += jnp.dot(moment, low, preferred_element_type=jnp.float32)
        total = part if total is None else total + part
    return total


def kernel(near_ref, far_ref, vel_ref, out_ref):
    beads, blocks = near_ref.shape[0], far_ref.shape[0]

    def one_bead(b, unused):
        pack = near_ref[b]
        centre = jnp.mean(pack, axis=1, keepdims=True)
        pos = scaled(pack, centre)
        near = near_operand(pos)

        def one_block(f, total):
            far = far_ref[f, b]
            left, right = far_operands(scaled(far, centre), far[3:4])
            return total + force_sums(left, right, near)

        total = lax.fori_loop(
            0, blocks, one_block, jnp.zeros((32, pack.shape[1]), jnp.float32)
        )
        sums = total[:8] + total[8:16] + total[16:24]
        force = (4.0 * KICK) * pack[3:4] * (pos * sums[3:4] - sums)
        out_ref[b] = vel_ref[b] + force[:3]
        return unused

    lax.fori_loop(0, beads, one_bead, 0)


def local(mode_pos, mode_vel, charges):
    local_beads = mode_pos.shape[0]
    own_modes = lax.axis_index("bead") * local_beads + jnp.arange(local_beads, dtype=jnp.int32)
    new_pos, new_vel = evolve(mode_pos, mode_vel, own_modes)
    both = lax.all_gather(jnp.concatenate((new_pos, new_vel), axis=1), "bead", axis=0, tiled=True)
    columns = jnp.arange(both.shape[0], dtype=jnp.int32)
    table = mode_table(own_modes[:, None], columns[None, :])
    mixed = jnp.einsum("bk,kcn->bcn", table, both, precision=HIGHEST)
    first, second = mixed[:, :3], mixed[:, 3:]
    count = charges.shape[0]
    charge_rows = jnp.broadcast_to(charges[None, None, :], (local_beads, 1, count))
    spare = jnp.zeros((local_beads, 4, count), jnp.float32)
    packed = jnp.concatenate((first, charge_rows, spare), axis=1)
    far = lax.all_gather(packed, "dom", axis=0)
    velocities = pl.pallas_call(
        kernel,
        out_shape=jax.ShapeDtypeStruct(first.shape, jnp.float32),
        in_specs=[pl.BlockSpec(memory_space=pltpu.VMEM)] * 3,
        out_specs=pl.BlockSpec(memory_space=pltpu.VMEM),
        compiler_params=pltpu.CompilerParams(vmem_limit_bytes=48 * 1024 * 1024),
    )(packed, far, second)
    return (first, velocities)


def solution(mesh):
    placed = (P("bead", None, "dom"), P("bead", None, "dom"), P("dom"))
    return jax.shard_map(
        local,
        mesh=mesh,
        in_specs=placed,
        out_specs=(P("bead", None, "dom"), P("bead", None, "dom")),
        check_vma=False,
    )
```

```python
import functools

import jax
import jax.numpy as jnp
import numpy as np
from jax import lax
from jax.experimental import pallas as pl
from jax.experimental.pallas import tpu as pltpu
from jax.sharding import PartitionSpec as P

KAPPA = 2.0
SOFTEN = 0.09
KICK = 0.3
OMEGA = 7.0
STEP_TIME = 0.1
LOG2E = 1.4426950408889634
ROWS = 256
MESH = pl.DeviceIdType.MESH


def mode_table(beads):
    bead, mode = np.arange(beads)[:, None], np.arange(beads)[None, :]
    angle = 2.0 * np.pi * bead * mode / beads
    wave = np.where(2 * mode < beads, np.cos(angle), np.sin(angle)) * np.sqrt(2.0 / beads)
    edge = np.where(mode == 0, 1.0, np.cos(np.pi * bead)) / np.sqrt(beads)
    return np.where((mode == 0) | (2 * mode == beads), edge, wave).astype(np.float32)


def step_table(beads):
    freq = 2.0 * OMEGA * np.sin(np.pi * np.arange(beads) / beads)
    theta = freq * STEP_TIME
    rate = np.where(freq > 0, np.sin(theta) / np.where(freq > 0, freq, 1.0), STEP_TIME)
    return np.stack((np.cos(theta), rate, -freq * np.sin(theta)), axis=1).astype(np.float32)


def split3(value):
    one = value.astype(jnp.bfloat16).astype(jnp.float32)
    rest = value - one
    two = rest.astype(jnp.bfloat16).astype(jnp.float32)
    return one, two, rest - two


def row_index(shape):
    return lax.broadcasted_iota(jnp.int32, shape, 0)


def scaled(pack, centre):
    return jnp.where(row_index(pack.shape) < 3, KAPPA * (pack - centre), 0.0)


def near_operand(pos):
    row = row_index(pos.shape)
    norm = jnp.sum(pos * pos, axis=0, keepdims=True) + KAPPA * KAPPA * SOFTEN
    one, two, three = split3(jnp.where(row == 3, norm, -2.0 * pos))
    last = row == 3
    groups = (
        one,
        jnp.where(last, two, one),
        jnp.where(last, three, two),
        jnp.where(last, 1.0, two),
        jnp.where(last, 1.0, one),
        jnp.where(last, 1.0, three),
    )
    return jnp.concatenate(groups, axis=0).astype(jnp.bfloat16)


def moment_parts(pos, charge):
    moments = jnp.where(row_index(pos.shape) == 3, charge, pos * charge)
    return jnp.concatenate(split3(moments) + (jnp.zeros_like(pos),), axis=0)


def far_operand(pos):
    last = row_index(pos.shape) == 3
    norm = jnp.sum(pos * pos, axis=0, keepdims=True)
    one, two, three = split3(jnp.where(last, norm, pos))
    first = jnp.where(last, 1.0, one)
    groups = (
        first,
        jnp.where(last, 1.0, two),
        first,
        jnp.where(last, one, two),
        jnp.where(last, two, three),
        jnp.where(last, three, one),
    )
    return jnp.concatenate(groups, axis=0).T.astype(jnp.bfloat16)


def pair_weight(square):
    inverse = lax.rsqrt(square)
    decay = jnp.exp2(square * (inverse * (-LOG2E)))
    return decay * (1.0 + inverse) * (inverse * inverse)


def block_sums(left, right, near, near_moment):
    total, backs = None, []
    for start in range(0, left.shape[0], ROWS):
        square = jnp.dot(left[start : start + ROWS], near, preferred_element_type=jnp.float32)
        weight = pair_weight(square)
        high = weight.astype(jnp.bfloat16)
        low = (weight - high.astype(jnp.float32)).astype(jnp.bfloat16)
        moment = right[:, start : start + ROWS]
        part = jnp.dot(moment, high, preferred_element_type=jnp.float32)
        part += jnp.dot(moment, low, preferred_element_type=jnp.float32)
        total = part if total is None else total + part
        if near_moment is not None:
            back = jnp.dot(high, near_moment, preferred_element_type=jnp.float32)
            back += jnp.dot(low, near_moment, preferred_element_type=jnp.float32)
            backs.append(back)
    back = jnp.concatenate(backs, axis=0).T if backs else None
    return total, back


def force_of(pos, charge, sums):
    sums = sums[:8] + sums[8:16] + sums[16:24]
    return (4.0 * KICK) * charge * (pos * sums[3:4] - sums)


def kernel(
    n_bead, n_dom, table_ref, step_ref, pos_ref, vel_ref, charge_ref, pos_out, vel_out,
    modes, packs, speed, centres, near_ops, near_moments, sums, backs, returned,
    mode_send, mode_recv, pack_send, pack_recv, back_send, back_recv,
):
    me_bead, me = lax.axis_index("bead"), lax.axis_index("dom")
    beads, half = pos_ref.shape[0], n_dom // 2
    part = beads // 2
    tile = (8, pos_ref.shape[2])
    row = row_index(tile)

    barrier = pltpu.get_barrier_semaphore()
    for step in range(1, n_bead):
        pl.semaphore_signal(
            barrier, inc=1, device_id={"bead": lax.rem(me_bead + step, n_bead)}, device_id_type=MESH
        )
    for step in range(1, n_dom):
        pl.semaphore_signal(
            barrier, inc=1, device_id={"dom": lax.rem(me + step, n_dom)}, device_id_type=MESH
        )

    for k in range(beads):
        mode = me_bead * beads + k
        old_pos, old_vel = pos_ref[k], vel_ref[k]
        modes[0, k] = jnp.zeros(tile, jnp.float32)
        modes[0, k, 0:3] = step_ref[mode, 0] * old_pos + step_ref[mode, 1] * old_vel
        modes[0, k, 4:7] = step_ref[mode, 2] * old_pos + step_ref[mode, 0] * old_vel
    pl.semaphore_wait(barrier, n_bead + n_dom - 2)

    def mode_copy(step):
        return pltpu.make_async_remote_copy(
            src_ref=modes.at[0], dst_ref=modes.at[step],
            send_sem=mode_send.at[step], recv_sem=mode_recv.at[step],
            device_id={"bead": lax.rem(me_bead + step, n_bead)}, device_id_type=MESH,
        )

    for step in range(1, n_bead):
        mode_copy(step).start()
    mixed = [jnp.zeros(tile, jnp.float32) for b in range(beads)]
    for step in range(n_bead):
        if step:
            mode_copy(step).wait_recv()
        first = lax.rem(me_bead - step + n_bead, n_bead) * beads
        for k in range(beads):
            mode = modes[step, k]
            for b in range(beads):
                mixed[b] = mixed[b] + table_ref[me_bead * beads + b, first + k] * mode

    charge = charge_ref[...]
    for b in range(beads):
        packs[0, b] = jnp.where(row < 3, mixed[b], jnp.where(row == 3, charge, 0.0))

    def pack_copy(step):
        return pltpu.make_async_remote_copy(
            src_ref=packs.at[0], dst_ref=packs.at[step],
            send_sem=pack_send.at[step], recv_sem=pack_recv.at[step],
            device_id={"dom": lax.rem(me + step, n_dom)}, device_id_type=MESH,
        )

    for step in range(1, half + 1):
        pack_copy(step).start()
    for b in range(beads):
        pos_out[b] = mixed[b][:3]
        speed[b] = pltpu.roll(mixed[b], 4, axis=0)
        pack = packs[0, b]
        centre = jnp.broadcast_to(jnp.mean(pack, axis=1, keepdims=True), tile)
        centres[b] = centre
        pos = scaled(pack, centre)
        near_ops[b] = near_operand(pos)
        near_moments[b] = moment_parts(pos, charge).T.astype(jnp.bfloat16)
        sums[b] = jnp.zeros((32, tile[1]), jnp.float32)

    def one_unit(step, b, with_back):
        pack = packs[step, b]
        pos = scaled(pack, centres[b])
        right = moment_parts(pos, pack[3:4]).astype(jnp.bfloat16)
        moment = near_moments[b] if with_back else None
        total, back = block_sums(far_operand(pos), right, near_ops[b], moment)
        sums[b] += total
        if with_back:
            backs[step, b] = force_of(pos, pack[3:4], back)

    def own_unit(b, unused):
        one_unit(0, b, False)
        return unused

    mine = jnp.where(me < half, 0, part)
    theirs = part - mine

    def back_copy(step):
        span = pl.ds(0, beads)
        return pltpu.make_async_remote_copy(
            src_ref=backs.at[step, span], dst_ref=returned.at[step, span],
            send_sem=back_send.at[step], recv_sem=back_recv.at[step],
            device_id={"dom": lax.rem(me - step + n_dom, n_dom)}, device_id_type=MESH,
        )

    def last_copy(first):
        span = pl.ds(first, part)
        return pltpu.make_async_remote_copy(
            src_ref=backs.at[half, span], dst_ref=returned.at[half, span],
            send_sem=back_send.at[half], recv_sem=back_recv.at[half],
            device_id={"dom": lax.rem(me - half + n_dom, n_dom)}, device_id_type=MESH,
        )

    lax.fori_loop(0, part, own_unit, 0)

    def one_step(step, unused):
        pack_copy(step).wait_recv()
        first = jnp.where(step < half, 0, mine)
        count = jnp.where(step < half, beads, part)

        def unit(b, inner):
            one_unit(step, first + b, True)
            return inner

        lax.fori_loop(0, count, unit, 0)

        @pl.when(step < half)
        def _():
            back_copy(step).start()

        return unused

    lax.fori_loop(1, half + 1, one_step, 0)
    last_copy(mine).start()
    lax.fori_loop(part, beads, own_unit, 0)

    for b in range(beads):
        pack = packs[0, b]
        pos = scaled(pack, centres[b])
        speed[b] += force_of(pos, pack[3:4], sums[b])

    def collect(step, unused):
        back_copy(step).wait_recv()
        for b in range(beads):
            speed[b] += returned[step, b]
        return unused

    lax.fori_loop(1, half, collect, 0)
    last_copy(theirs).wait_recv()
    for b in range(part):
        speed[theirs + b] += returned[half, theirs + b]
    for b in range(beads):
        vel_out[b] = speed[b, 0:3]

    for step in range(1, n_bead):
        mode_copy(step).wait_send()
    for step in range(1, half + 1):
        pack_copy(step).wait_send()
    for step in range(1, half):
        back_copy(step).wait_send()
    last_copy(mine).wait_send()


def local(mode_pos, mode_vel, charges):
    n_bead, n_dom = lax.axis_size("bead"), lax.axis_size("dom")
    beads, unused, count = mode_pos.shape
    half = n_dom // 2
    total = n_bead * beads
    vmem, smem = pl.BlockSpec(memory_space=pltpu.VMEM), pl.BlockSpec(memory_space=pltpu.SMEM)
    shape = jax.ShapeDtypeStruct(mode_pos.shape, jnp.float32)
    return pl.pallas_call(
        functools.partial(kernel, n_bead, n_dom),
        out_shape=(shape, shape),
        in_specs=[smem, smem, vmem, vmem, vmem],
        out_specs=(vmem, vmem),
        scratch_shapes=[
            pltpu.VMEM((n_bead, beads, 8, count), jnp.float32),
            pltpu.VMEM((half + 1, beads, 8, count), jnp.float32),
            pltpu.VMEM((beads, 8, count), jnp.float32),
            pltpu.VMEM((beads, 8, count), jnp.float32),
            pltpu.VMEM((beads, 48, count), jnp.bfloat16),
            pltpu.VMEM((beads, count, 32), jnp.bfloat16),
            pltpu.VMEM((beads, 32, count), jnp.float32),
            pltpu.VMEM((half + 1, beads, 8, count), jnp.float32),
            pltpu.VMEM((half + 1, beads, 8, count), jnp.float32),
            pltpu.SemaphoreType.DMA((n_bead,)),
            pltpu.SemaphoreType.DMA((n_bead,)),
            pltpu.SemaphoreType.DMA((half + 1,)),
            pltpu.SemaphoreType.DMA((half + 1,)),
            pltpu.SemaphoreType.DMA((half + 1,)),
            pltpu.SemaphoreType.DMA((half + 1,)),
        ],
        compiler_params=pltpu.CompilerParams(
            collective_id=0, has_side_effects=True, vmem_limit_bytes=48 * 1024 * 1024
        ),
    )(mode_table(total), step_table(total), mode_pos, mode_vel, charges[None])


def solution(mesh):
    placed = (P("bead", None, "dom"), P("bead", None, "dom"), P("dom"))
    return jax.shard_map(
        local,
        mesh=mesh,
        in_specs=placed,
        out_specs=(P("bead", None, "dom"), P("bead", None, "dom")),
        check_vma=False,
    )
```

```python
import functools

import jax
import jax.numpy as jnp
import numpy as np
from jax import lax
from jax.experimental import pallas as pl
from jax.experimental.pallas import tpu as pltpu
from jax.sharding import PartitionSpec as P

KAPPA = 2.0
SOFTEN = 0.09
KICK = 0.3
OMEGA = 7.0
STEP_TIME = 0.1
LOG2E = 1.4426950408889634
ROWS = 256
STRIP = 16
MESH = pl.DeviceIdType.MESH


def mode_table(beads):
    bead, mode = np.arange(beads)[:, None], np.arange(beads)[None, :]
    angle = 2.0 * np.pi * bead * mode / beads
    wave = np.where(2 * mode < beads, np.cos(angle), np.sin(angle)) * np.sqrt(2.0 / beads)
    edge = np.where(mode == 0, 1.0, np.cos(np.pi * bead)) / np.sqrt(beads)
    return np.where((mode == 0) | (2 * mode == beads), edge, wave).astype(np.float32)


def step_table(beads):
    freq = 2.0 * OMEGA * np.sin(np.pi * np.arange(beads) / beads)
    theta = freq * STEP_TIME
    rate = np.where(freq > 0, np.sin(theta) / np.where(freq > 0, freq, 1.0), STEP_TIME)
    return np.stack((np.cos(theta), rate, -freq * np.sin(theta)), axis=1).astype(np.float32)


def split3(value):
    one = value.astype(jnp.bfloat16).astype(jnp.float32)
    rest = value - one
    two = rest.astype(jnp.bfloat16).astype(jnp.float32)
    return one, two, rest - two


def row_index(shape):
    return lax.broadcasted_iota(jnp.int32, shape, 0)


def scaled(pack, centre):
    return jnp.where(row_index(pack.shape) < 3, KAPPA * (pack - centre), 0.0)


def near_operand(pos):
    row = row_index(pos.shape)
    norm = jnp.sum(pos * pos, axis=0, keepdims=True) + KAPPA * KAPPA * SOFTEN
    one, two, three = split3(jnp.where(row == 3, norm, -2.0 * pos))
    last = row == 3
    groups = (
        one,
        jnp.where(last, two, one),
        jnp.where(last, three, two),
        jnp.where(last, 1.0, two),
        jnp.where(last, 1.0, one),
        jnp.where(last, 1.0, three),
    )
    return jnp.concatenate(groups, axis=0).astype(jnp.bfloat16)


def moment_parts(pos, charge):
    moments = jnp.where(row_index(pos.shape) == 3, charge, pos * charge)
    return jnp.concatenate(split3(moments) + (jnp.zeros_like(pos),), axis=0)


def far_operand(pos):
    last = row_index(pos.shape) == 3
    norm = jnp.sum(pos * pos, axis=0, keepdims=True)
    one, two, three = split3(jnp.where(last, norm, pos))
    first = jnp.where(last, 1.0, one)
    groups = (
        first,
        jnp.where(last, 1.0, two),
        first,
        jnp.where(last, one, two),
        jnp.where(last, two, three),
        jnp.where(last, three, one),
    )
    return jnp.concatenate(groups, axis=0).T.astype(jnp.bfloat16)


def pair_weight(square):
    inverse = lax.rsqrt(square)
    decay = jnp.exp2(square * (inverse * (-LOG2E)))
    return decay * (1.0 + inverse) * (inverse * inverse)


def block_sums(left, right, near, near_moment, squares, weights):
    far_count, count = squares.shape
    total, backs = None, []
    for start in range(0, far_count, ROWS):
        squares[start : start + ROWS] = jnp.dot(
            left[start : start + ROWS], near, preferred_element_type=jnp.float32
        )
    for start in range(0, far_count, ROWS):
        for strip in range(start, start + ROWS, STRIP):
            weight = pair_weight(squares[strip : strip + STRIP])
            high = weight.astype(jnp.bfloat16)
            low = (weight - high.astype(jnp.float32)).astype(jnp.bfloat16)
            weights[strip : strip + STRIP, :count] = high
            weights[strip : strip + STRIP, count:] = low
        moment = right[:, start : start + ROWS]
        high, low = weights[start : start + ROWS, :count], weights[start : start + ROWS, count:]
        part = jnp.dot(moment, high, preferred_element_type=jnp.float32)
        part += jnp.dot(moment, low, preferred_element_type=jnp.float32)
        total = part if total is None else total + part
        if near_moment is not None:
            both = weights[start : start + ROWS]
            backs.append(jnp.dot(both, near_moment, preferred_element_type=jnp.float32))
    back = jnp.concatenate(backs, axis=0).T if backs else None
    return total, back


def force_of(pos, charge, sums):
    sums = sums[:8] + sums[8:16] + sums[16:24]
    return (4.0 * KICK) * charge * (pos * sums[3:4] - sums)


def kernel(
    n_bead, n_dom, table_ref, step_ref, pos_ref, vel_ref, charge_ref, pos_out, vel_out,
    modes, packs, speed, centres, near_ops, near_moments, sums, backs, returned, squares, weights,
    mode_send, mode_recv, pack_send, pack_recv, back_send, back_recv,
):
    me_bead, me = lax.axis_index("bead"), lax.axis_index("dom")
    beads, half = pos_ref.shape[0], n_dom // 2
    part = beads // 2
    tile = (8, pos_ref.shape[2])
    row = row_index(tile)

    barrier = pltpu.get_barrier_semaphore()
    for step in range(1, n_bead):
        pl.semaphore_signal(
            barrier, inc=1, device_id={"bead": lax.rem(me_bead + step, n_bead)}, device_id_type=MESH
        )
    for step in range(1, n_dom):
        pl.semaphore_signal(
            barrier, inc=1, device_id={"dom": lax.rem(me + step, n_dom)}, device_id_type=MESH
        )

    for k in range(beads):
        mode = me_bead * beads + k
        old_pos, old_vel = pos_ref[k], vel_ref[k]
        modes[0, k] = jnp.zeros(tile, jnp.float32)
        modes[0, k, 0:3] = step_ref[mode, 0] * old_pos + step_ref[mode, 1] * old_vel
        modes[0, k, 4:7] = step_ref[mode, 2] * old_pos + step_ref[mode, 0] * old_vel
    pl.semaphore_wait(barrier, n_bead + n_dom - 2)

    def mode_copy(step):
        return pltpu.make_async_remote_copy(
            src_ref=modes.at[0], dst_ref=modes.at[step],
            send_sem=mode_send.at[step], recv_sem=mode_recv.at[step],
            device_id={"bead": lax.rem(me_bead + step, n_bead)}, device_id_type=MESH,
        )

    for step in range(1, n_bead):
        mode_copy(step).start()
    mixed = [jnp.zeros(tile, jnp.float32) for b in range(beads)]
    for step in range(n_bead):
        if step:
            mode_copy(step).wait_recv()
        first = lax.rem(me_bead - step + n_bead, n_bead) * beads
        for k in range(beads):
            mode = modes[step, k]
            for b in range(beads):
                mixed[b] = mixed[b] + table_ref[me_bead * beads + b, first + k] * mode

    charge = charge_ref[...]
    for b in range(beads):
        packs[0, b] = jnp.where(row < 3, mixed[b], jnp.where(row == 3, charge, 0.0))

    def pack_copy(step):
        return pltpu.make_async_remote_copy(
            src_ref=packs.at[0], dst_ref=packs.at[step],
            send_sem=pack_send.at[step], recv_sem=pack_recv.at[step],
            device_id={"dom": lax.rem(me + step, n_dom)}, device_id_type=MESH,
        )

    for step in range(1, half + 1):
        pack_copy(step).start()
    for b in range(beads):
        pos_out[b] = mixed[b][:3]
        speed[b] = pltpu.roll(mixed[b], 4, axis=0)
        pack = packs[0, b]
        centre = jnp.broadcast_to(jnp.mean(pack, axis=1, keepdims=True), tile)
        centres[b] = centre
        pos = scaled(pack, centre)
        near_ops[b] = near_operand(pos)
        moment = moment_parts(pos, charge).T.astype(jnp.bfloat16)
        near_moments[b] = jnp.concatenate((moment, moment), axis=0)
        sums[b] = jnp.zeros((32, tile[1]), jnp.float32)

    def one_unit(step, b, with_back):
        pack = packs[step, b]
        pos = scaled(pack, centres[b])
        right = moment_parts(pos, pack[3:4]).astype(jnp.bfloat16)
        moment = near_moments[b] if with_back else None
        total, back = block_sums(
            far_operand(pos), right, near_ops[b], moment, squares, weights
        )
        sums[b] += total
        if with_back:
            backs[step, b] = force_of(pos, pack[3:4], back)

    def own_unit(b, unused):
        one_unit(0, b, False)
        return unused

    mine = jnp.where(me < half, 0, part)
    theirs = part - mine

    def back_copy(step):
        span = pl.ds(0, beads)
        return pltpu.make_async_remote_copy(
            src_ref=backs.at[step, span], dst_ref=returned.at[step, span],
            send_sem=back_send.at[step], recv_sem=back_recv.at[step],
            device_id={"dom": lax.rem(me - step + n_dom, n_dom)}, device_id_type=MESH,
        )

    def last_copy(first):
        span = pl.ds(first, part)
        return pltpu.make_async_remote_copy(
            src_ref=backs.at[half, span], dst_ref=returned.at[half, span],
            send_sem=back_send.at[half], recv_sem=back_recv.at[half],
            device_id={"dom": lax.rem(me - half + n_dom, n_dom)}, device_id_type=MESH,
        )

    lax.fori_loop(0, part, own_unit, 0)

    def one_step(step, unused):
        pack_copy(step).wait_recv()
        first = jnp.where(step < half, 0, mine)
        count = jnp.where(step < half, beads, part)

        def unit(b, inner):
            one_unit(step, first + b, True)
            return inner

        lax.fori_loop(0, count, unit, 0)

        @pl.when(step < half)
        def _():
            back_copy(step).start()

        return unused

    lax.fori_loop(1, half + 1, one_step, 0)
    last_copy(mine).start()
    lax.fori_loop(part, beads, own_unit, 0)

    for b in range(beads):
        pack = packs[0, b]
        pos = scaled(pack, centres[b])
        speed[b] += force_of(pos, pack[3:4], sums[b])

    def collect(step, unused):
        back_copy(step).wait_recv()
        for b in range(beads):
            speed[b] += returned[step, b]
        return unused

    lax.fori_loop(1, half, collect, 0)
    last_copy(theirs).wait_recv()
    for b in range(part):
        speed[theirs + b] += returned[half, theirs + b]
    for b in range(beads):
        vel_out[b] = speed[b, 0:3]

    for step in range(1, n_bead):
        mode_copy(step).wait_send()
    for step in range(1, half + 1):
        pack_copy(step).wait_send()
    for step in range(1, half):
        back_copy(step).wait_send()
    last_copy(mine).wait_send()


def local(mode_pos, mode_vel, charges):
    n_bead, n_dom = lax.axis_size("bead"), lax.axis_size("dom")
    beads, unused, count = mode_pos.shape
    half = n_dom // 2
    total = n_bead * beads
    vmem, smem = pl.BlockSpec(memory_space=pltpu.VMEM), pl.BlockSpec(memory_space=pltpu.SMEM)
    shape = jax.ShapeDtypeStruct(mode_pos.shape, jnp.float32)
    return pl.pallas_call(
        functools.partial(kernel, n_bead, n_dom),
        out_shape=(shape, shape),
        in_specs=[smem, smem, vmem, vmem, vmem],
        out_specs=(vmem, vmem),
        scratch_shapes=[
            pltpu.VMEM((n_bead, beads, 8, count), jnp.float32),
            pltpu.VMEM((half + 1, beads, 8, count), jnp.float32),
            pltpu.VMEM((beads, 8, count), jnp.float32),
            pltpu.VMEM((beads, 8, count), jnp.float32),
            pltpu.VMEM((beads, 48, count), jnp.bfloat16),
            pltpu.VMEM((beads, 2 * count, 32), jnp.bfloat16),
            pltpu.VMEM((beads, 32, count), jnp.float32),
            pltpu.VMEM((half + 1, beads, 8, count), jnp.float32),
            pltpu.VMEM((half + 1, beads, 8, count), jnp.float32),
            pltpu.VMEM((count, count), jnp.float32),
            pltpu.VMEM((count, 2 * count), jnp.bfloat16),
            pltpu.SemaphoreType.DMA((n_bead,)),
            pltpu.SemaphoreType.DMA((n_bead,)),
            pltpu.SemaphoreType.DMA((half + 1,)),
            pltpu.SemaphoreType.DMA((half + 1,)),
            pltpu.SemaphoreType.DMA((half + 1,)),
            pltpu.SemaphoreType.DMA((half + 1,)),
        ],
        compiler_params=pltpu.CompilerParams(
            collective_id=0, has_side_effects=True, vmem_limit_bytes=48 * 1024 * 1024
        ),
    )(mode_table(total), step_table(total), mode_pos, mode_vel, charges[None])


def solution(mesh):
    placed = (P("bead", None, "dom"), P("bead", None, "dom"), P("dom"))
    return jax.shard_map(
        local,
        mesh=mesh,
        in_specs=placed,
        out_specs=(P("bead", None, "dom"), P("bead", None, "dom")),
        check_vma=False,
    )
```

```python
import functools

import jax
import jax.numpy as jnp
import numpy as np
from jax import lax
from jax.experimental import pallas as pl
from jax.experimental.pallas import tpu as pltpu
from jax.sharding import PartitionSpec as P

KAPPA = 2.0
SOFTEN = 0.09
KICK = 0.3
OMEGA = 7.0
STEP_TIME = 0.1
LOG2E = 1.4426950408889634
ROWS = 256
STRIP = 16
MESH = pl.DeviceIdType.MESH


def mode_table(beads):
    bead, mode = np.arange(beads)[:, None], np.arange(beads)[None, :]
    angle = 2.0 * np.pi * bead * mode / beads
    wave = np.where(2 * mode < beads, np.cos(angle), np.sin(angle)) * np.sqrt(2.0 / beads)
    edge = np.where(mode == 0, 1.0, np.cos(np.pi * bead)) / np.sqrt(beads)
    return np.where((mode == 0) | (2 * mode == beads), edge, wave).astype(np.float32)


def step_table(beads):
    freq = 2.0 * OMEGA * np.sin(np.pi * np.arange(beads) / beads)
    theta = freq * STEP_TIME
    rate = np.where(freq > 0, np.sin(theta) / np.where(freq > 0, freq, 1.0), STEP_TIME)
    return np.stack((np.cos(theta), rate, -freq * np.sin(theta)), axis=1).astype(np.float32)


def split3(value):
    one = value.astype(jnp.bfloat16).astype(jnp.float32)
    rest = value - one
    two = rest.astype(jnp.bfloat16).astype(jnp.float32)
    return one, two, rest - two


def row_index(shape):
    return lax.broadcasted_iota(jnp.int32, shape, 0)


def scaled(pack, centre):
    return jnp.where(row_index(pack.shape) < 3, KAPPA * (pack - centre), 0.0)


def near_operand(pos):
    row = row_index(pos.shape)
    norm = jnp.sum(pos * pos, axis=0, keepdims=True) + KAPPA * KAPPA * SOFTEN
    one, two, three = split3(jnp.where(row == 3, norm, -2.0 * pos))
    last = row == 3
    groups = (
        one,
        jnp.where(last, two, one),
        jnp.where(last, three, two),
        jnp.where(last, 1.0, two),
        jnp.where(last, 1.0, one),
        jnp.where(last, 1.0, three),
    )
    return jnp.concatenate(groups, axis=0).astype(jnp.bfloat16)


def moment_parts(pos, charge):
    moments = jnp.where(row_index(pos.shape) == 3, charge, pos * charge)
    return jnp.concatenate(split3(moments) + (jnp.zeros_like(pos),), axis=0)


def far_operand(pos):
    last = row_index(pos.shape) == 3
    norm = jnp.sum(pos * pos, axis=0, keepdims=True)
    one, two, three = split3(jnp.where(last, norm, pos))
    first = jnp.where(last, 1.0, one)
    groups = (
        first,
        jnp.where(last, 1.0, two),
        first,
        jnp.where(last, one, two),
        jnp.where(last, two, three),
        jnp.where(last, three, one),
    )
    return jnp.concatenate(groups, axis=0).T.astype(jnp.bfloat16)


def pair_weight(square):
    inverse = lax.rsqrt(square)
    decay = jnp.exp2(square * (inverse * (-LOG2E)))
    return decay * (1.0 + inverse) * (inverse * inverse)


def square_rows(start, left, near, squares):
    rows = pl.ds(start, ROWS)
    squares[rows] = jnp.dot(left[rows], near[...], preferred_element_type=jnp.float32)


def weigh_rows(start, squares, weights):
    count = squares.shape[1]
    for strip in range(start, start + ROWS, STRIP):
        weight = pair_weight(squares[strip : strip + STRIP])
        high = weight.astype(jnp.bfloat16)
        low = (weight - high.astype(jnp.float32)).astype(jnp.bfloat16)
        weights[strip : strip + STRIP, :count] = high
        weights[strip : strip + STRIP, count:] = low


def near_sums(start, right, weights):
    rows, count = pl.ds(start, ROWS), weights.shape[1] // 2
    moment = right[:, rows]
    high = jnp.dot(moment, weights[rows, :count], preferred_element_type=jnp.float32)
    return high + jnp.dot(moment, weights[rows, count:], preferred_element_type=jnp.float32)


def far_sums(start, near_moment, weights, back):
    rows = pl.ds(start, ROWS)
    back[rows] = jnp.dot(weights[rows], near_moment[...], preferred_element_type=jnp.float32)


def force_of(pos, charge, sums):
    sums = sums[:8] + sums[8:16] + sums[16:24]
    return (4.0 * KICK) * charge * (pos * sums[3:4] - sums)


def kernel(
    n_bead, n_dom, table_ref, step_ref, pos_ref, vel_ref, charge_ref, pos_out, vel_out,
    modes, packs, speed, centres, near_ops, near_moments, sums, backs, returned, squares, weights,
    lefts, rights, raw_backs, mode_send, mode_recv, pack_send, pack_recv, back_send, back_recv,
):
    me_bead, me = lax.axis_index("bead"), lax.axis_index("dom")
    beads, half = pos_ref.shape[0], n_dom // 2
    part = beads // 2
    group = squares.shape[0]
    tile = (8, pos_ref.shape[2])
    row = row_index(tile)

    barrier = pltpu.get_barrier_semaphore()
    for step in range(1, n_bead):
        pl.semaphore_signal(
            barrier, inc=1, device_id={"bead": lax.rem(me_bead + step, n_bead)}, device_id_type=MESH
        )
    for step in range(1, n_dom):
        pl.semaphore_signal(
            barrier, inc=1, device_id={"dom": lax.rem(me + step, n_dom)}, device_id_type=MESH
        )

    for k in range(beads):
        mode = me_bead * beads + k
        old_pos, old_vel = pos_ref[k], vel_ref[k]
        modes[0, k] = jnp.zeros(tile, jnp.float32)
        modes[0, k, 0:3] = step_ref[mode, 0] * old_pos + step_ref[mode, 1] * old_vel
        modes[0, k, 4:7] = step_ref[mode, 2] * old_pos + step_ref[mode, 0] * old_vel
    pl.semaphore_wait(barrier, n_bead + n_dom - 2)

    def mode_copy(step):
        return pltpu.make_async_remote_copy(
            src_ref=modes.at[0], dst_ref=modes.at[step],
            send_sem=mode_send.at[step], recv_sem=mode_recv.at[step],
            device_id={"bead": lax.rem(me_bead + step, n_bead)}, device_id_type=MESH,
        )

    for step in range(1, n_bead):
        mode_copy(step).start()
    mixed = [jnp.zeros(tile, jnp.float32) for b in range(beads)]
    for step in range(n_bead):
        if step:
            mode_copy(step).wait_recv()
        first = lax.rem(me_bead - step + n_bead, n_bead) * beads
        for k in range(beads):
            mode = modes[step, k]
            for b in range(beads):
                mixed[b] = mixed[b] + table_ref[me_bead * beads + b, first + k] * mode

    charge = charge_ref[...]
    for b in range(beads):
        packs[0, b] = jnp.where(row < 3, mixed[b], jnp.where(row == 3, charge, 0.0))

    def pack_copy(step):
        return pltpu.make_async_remote_copy(
            src_ref=packs.at[0], dst_ref=packs.at[step],
            send_sem=pack_send.at[step], recv_sem=pack_recv.at[step],
            device_id={"dom": lax.rem(me + step, n_dom)}, device_id_type=MESH,
        )

    for step in range(1, half + 1):
        pack_copy(step).start()
    for b in range(beads):
        pos_out[b] = mixed[b][:3]
        speed[b] = pltpu.roll(mixed[b], 4, axis=0)
        pack = packs[0, b]
        centre = jnp.broadcast_to(jnp.mean(pack, axis=1, keepdims=True), tile)
        centres[b] = centre
        pos = scaled(pack, centre)
        near_ops[b] = near_operand(pos)
        moment = moment_parts(pos, charge).T.astype(jnp.bfloat16)
        near_moments[b] = jnp.concatenate((moment, moment), axis=0)
        sums[b] = jnp.zeros((32, tile[1]), jnp.float32)

    def prepare(step):
        for b in range(beads):
            pack = packs[step, b]
            pos = scaled(pack, centres[b])
            lefts[b] = far_operand(pos)
            rights[b] = moment_parts(pos, pack[3:4]).astype(jnp.bfloat16)

    def some_beads(first, with_back):
        starts = range(0, tile[1], ROWS)
        for start in starts:
            square_rows(start, lefts.at[first], near_ops.at[first], squares.at[0])
        for i in range(group):
            b = first + i
            total = sums[b]
            for start in starts:
                weigh_rows(start, squares.at[i], weights.at[i])
                if i + 1 < group:
                    square_rows(start, lefts.at[b + 1], near_ops.at[b + 1], squares.at[i + 1])
                total += near_sums(start, rights.at[b], weights.at[i])
                if with_back:
                    far_sums(start, near_moments.at[b], weights.at[i], raw_backs.at[b])
            sums[b] = total

    def own_beads(g, unused):
        some_beads(g * group, False)
        return unused

    mine = jnp.where(me < half, 0, part)
    theirs = part - mine

    def back_copy(step):
        span = pl.ds(0, beads)
        return pltpu.make_async_remote_copy(
            src_ref=backs.at[step, span], dst_ref=returned.at[step, span],
            send_sem=back_send.at[step], recv_sem=back_recv.at[step],
            device_id={"dom": lax.rem(me - step + n_dom, n_dom)}, device_id_type=MESH,
        )

    def last_copy(first):
        span = pl.ds(first, part)
        return pltpu.make_async_remote_copy(
            src_ref=backs.at[half, span], dst_ref=returned.at[half, span],
            send_sem=back_send.at[half], recv_sem=back_recv.at[half],
            device_id={"dom": lax.rem(me - half + n_dom, n_dom)}, device_id_type=MESH,
        )

    prepare(0)
    lax.fori_loop(0, part // group, own_beads, 0)

    def one_step(step, unused):
        pack_copy(step).wait_recv()
        prepare(step)
        first = jnp.where(step < half, 0, mine)
        count = jnp.where(step < half, beads // group, part // group)

        def unit(g, inner):
            some_beads(first + g * group, True)
            return inner

        lax.fori_loop(0, count, unit, 0)
        for b in range(beads):
            pack = packs[step, b]
            backs[step, b] = force_of(scaled(pack, centres[b]), pack[3:4], raw_backs[b].T)

        @pl.when(step < half)
        def _():
            back_copy(step).start()

        return unused

    lax.fori_loop(1, half + 1, one_step, 0)
    last_copy(mine).start()
    prepare(0)
    lax.fori_loop(part // group, beads // group, own_beads, 0)

    for b in range(beads):
        pack = packs[0, b]
        pos = scaled(pack, centres[b])
        speed[b] += force_of(pos, pack[3:4], sums[b])

    def collect(step, unused):
        back_copy(step).wait_recv()
        for b in range(beads):
            speed[b] += returned[step, b]
        return unused

    lax.fori_loop(1, half, collect, 0)
    last_copy(theirs).wait_recv()
    for b in range(part):
        speed[theirs + b] += returned[half, theirs + b]
    for b in range(beads):
        vel_out[b] = speed[b, 0:3]

    for step in range(1, n_bead):
        mode_copy(step).wait_send()
    for step in range(1, half + 1):
        pack_copy(step).wait_send()
    for step in range(1, half):
        back_copy(step).wait_send()
    last_copy(mine).wait_send()


def local(mode_pos, mode_vel, charges):
    n_bead, n_dom = lax.axis_size("bead"), lax.axis_size("dom")
    beads, unused, count = mode_pos.shape
    half = n_dom // 2
    total = n_bead * beads
    group = 2 if beads % 4 == 0 else 1
    vmem, smem = pl.BlockSpec(memory_space=pltpu.VMEM), pl.BlockSpec(memory_space=pltpu.SMEM)
    shape = jax.ShapeDtypeStruct(mode_pos.shape, jnp.float32)
    return pl.pallas_call(
        functools.partial(kernel, n_bead, n_dom),
        out_shape=(shape, shape),
        in_specs=[smem, smem, vmem, vmem, vmem],
        out_specs=(vmem, vmem),
        scratch_shapes=[
            pltpu.VMEM((n_bead, beads, 8, count), jnp.float32),
            pltpu.VMEM((half + 1, beads, 8, count), jnp.float32),
            pltpu.VMEM((beads, 8, count), jnp.float32),
            pltpu.VMEM((beads, 8, count), jnp.float32),
            pltpu.VMEM((beads, 48, count), jnp.bfloat16),
            pltpu.VMEM((beads, 2 * count, 32), jnp.bfloat16),
            pltpu.VMEM((beads, 32, count), jnp.float32),
            pltpu.VMEM((half + 1, beads, 8, count), jnp.float32),
            pltpu.VMEM((half + 1, beads, 8, count), jnp.float32),
            pltpu.VMEM((group, count, count), jnp.float32),
            pltpu.VMEM((group, count, 2 * count), jnp.bfloat16),
            pltpu.VMEM((beads, count, 48), jnp.bfloat16),
            pltpu.VMEM((beads, 32, count), jnp.bfloat16),
            pltpu.VMEM((beads, count, 32), jnp.float32),
            pltpu.SemaphoreType.DMA((n_bead,)),
            pltpu.SemaphoreType.DMA((n_bead,)),
            pltpu.SemaphoreType.DMA((half + 1,)),
            pltpu.SemaphoreType.DMA((half + 1,)),
            pltpu.SemaphoreType.DMA((half + 1,)),
            pltpu.SemaphoreType.DMA((half + 1,)),
        ],
        compiler_params=pltpu.CompilerParams(
            collective_id=0, has_side_effects=True, vmem_limit_bytes=48 * 1024 * 1024
        ),
    )(mode_table(total), step_table(total), mode_pos, mode_vel, charges[None])


def solution(mesh):
    placed = (P("bead", None, "dom"), P("bead", None, "dom"), P("dom"))
    return jax.shard_map(
        local,
        mesh=mesh,
        in_specs=placed,
        out_specs=(P("bead", None, "dom"), P("bead", None, "dom")),
        check_vma=False,
    )
```

```python
import functools

import jax
import jax.numpy as jnp
import numpy as np
from jax import lax
from jax.experimental import pallas as pl
from jax.experimental.pallas import tpu as pltpu
from jax.sharding import PartitionSpec as P

KAPPA = 2.0
SOFTEN = 0.09
KICK = 0.3
OMEGA = 7.0
STEP_TIME = 0.1
LOG2E = 1.4426950408889634
ROWS = 256
STRIP = 16
MESH = pl.DeviceIdType.MESH


def mode_table(beads):
    bead, mode = np.arange(beads)[:, None], np.arange(beads)[None, :]
    angle = 2.0 * np.pi * bead * mode / beads
    wave = np.where(2 * mode < beads, np.cos(angle), np.sin(angle)) * np.sqrt(2.0 / beads)
    edge = np.where(mode == 0, 1.0, np.cos(np.pi * bead)) / np.sqrt(beads)
    return np.where((mode == 0) | (2 * mode == beads), edge, wave).astype(np.float32)


def step_table(beads):
    freq = 2.0 * OMEGA * np.sin(np.pi * np.arange(beads) / beads)
    theta = freq * STEP_TIME
    rate = np.where(freq > 0, np.sin(theta) / np.where(freq > 0, freq, 1.0), STEP_TIME)
    return np.stack((np.cos(theta), rate, -freq * np.sin(theta)), axis=1).astype(np.float32)


def split3(value):
    one = value.astype(jnp.bfloat16).astype(jnp.float32)
    rest = value - one
    two = rest.astype(jnp.bfloat16).astype(jnp.float32)
    return one, two, rest - two


def row_index(shape):
    return lax.broadcasted_iota(jnp.int32, shape, 0)


def scaled(pack, centre):
    return jnp.where(row_index(pack.shape) < 3, KAPPA * (pack - centre), 0.0)


def near_operand(pos):
    row = row_index(pos.shape)
    norm = jnp.sum(pos * pos, axis=0, keepdims=True) + KAPPA * KAPPA * SOFTEN
    one, two, three = split3(jnp.where(row == 3, norm, -2.0 * pos))
    last = row == 3
    groups = (
        one,
        jnp.where(last, two, one),
        jnp.where(last, three, two),
        jnp.where(last, 1.0, two),
        jnp.where(last, 1.0, one),
        jnp.where(last, 1.0, three),
    )
    return jnp.concatenate(groups, axis=0).astype(jnp.bfloat16)


def moment_parts(pos, charge):
    moments = jnp.where(row_index(pos.shape) == 3, charge, pos * charge)
    return jnp.concatenate(split3(moments) + (jnp.zeros_like(pos),), axis=0)


def far_operand(pos):
    last = row_index(pos.shape) == 3
    norm = jnp.sum(pos * pos, axis=0, keepdims=True)
    one, two, three = split3(jnp.where(last, norm, pos))
    first = jnp.where(last, 1.0, one)
    groups = (
        first,
        jnp.where(last, 1.0, two),
        first,
        jnp.where(last, one, two),
        jnp.where(last, two, three),
        jnp.where(last, three, one),
    )
    return jnp.concatenate(groups, axis=0).T.astype(jnp.bfloat16)


def pair_weight(square):
    inverse = lax.rsqrt(square)
    decay = jnp.exp2(square * (inverse * (-LOG2E)))
    return decay * (1.0 + inverse) * (inverse * inverse)


def square_rows(left, near, squares):
    squares[...] = jnp.dot(left[...], near[...], preferred_element_type=jnp.float32)


def weigh_rows(start, squares, weights):
    count = squares.shape[1]
    for strip in range(start, start + ROWS, STRIP):
        weight = pair_weight(squares[strip : strip + STRIP])
        high = weight.astype(jnp.bfloat16)
        low = (weight - high.astype(jnp.float32)).astype(jnp.bfloat16)
        weights[strip : strip + STRIP, :count] = high
        weights[strip : strip + STRIP, count:] = low


def near_sums(start, right, weights):
    rows, count = pl.ds(start, ROWS), weights.shape[1] // 2
    moment = right[:, rows]
    high = jnp.dot(moment, weights[rows, :count], preferred_element_type=jnp.float32)
    return high + jnp.dot(moment, weights[rows, count:], preferred_element_type=jnp.float32)


def far_sums(near_moment, weights, back):
    back[...] = jnp.dot(weights[...], near_moment[...], preferred_element_type=jnp.float32)


def force_of(pos, charge, sums):
    sums = sums[:8] + sums[8:16] + sums[16:24]
    return (4.0 * KICK) * charge * (pos * sums[3:4] - sums)


def kernel(
    n_bead, n_dom, table_ref, step_ref, pos_ref, vel_ref, charge_ref, pos_out, vel_out,
    modes, packs, speed, centres, near_ops, near_moments, sums, backs, returned, squares, weights,
    lefts, rights, raw_backs, mode_send, mode_recv, pack_send, pack_recv, back_send, back_recv,
):
    me_bead, me = lax.axis_index("bead"), lax.axis_index("dom")
    beads, half = pos_ref.shape[0], n_dom // 2
    part = beads // 2
    group = squares.shape[0]
    tile = (8, pos_ref.shape[2])
    row = row_index(tile)

    barrier = pltpu.get_barrier_semaphore()
    for step in range(1, n_bead):
        pl.semaphore_signal(
            barrier, inc=1, device_id={"bead": lax.rem(me_bead + step, n_bead)}, device_id_type=MESH
        )
    for step in range(1, n_dom):
        pl.semaphore_signal(
            barrier, inc=1, device_id={"dom": lax.rem(me + step, n_dom)}, device_id_type=MESH
        )

    for k in range(beads):
        mode = me_bead * beads + k
        old_pos, old_vel = pos_ref[k], vel_ref[k]
        modes[0, k] = jnp.zeros(tile, jnp.float32)
        modes[0, k, 0:3] = step_ref[mode, 0] * old_pos + step_ref[mode, 1] * old_vel
        modes[0, k, 4:7] = step_ref[mode, 2] * old_pos + step_ref[mode, 0] * old_vel
    pl.semaphore_wait(barrier, n_bead + n_dom - 2)

    def mode_copy(step):
        return pltpu.make_async_remote_copy(
            src_ref=modes.at[0], dst_ref=modes.at[step],
            send_sem=mode_send.at[step], recv_sem=mode_recv.at[step],
            device_id={"bead": lax.rem(me_bead + step, n_bead)}, device_id_type=MESH,
        )

    for step in range(1, n_bead):
        mode_copy(step).start()
    mixed = [jnp.zeros(tile, jnp.float32) for b in range(beads)]
    for step in range(n_bead):
        if step:
            mode_copy(step).wait_recv()
        first = lax.rem(me_bead - step + n_bead, n_bead) * beads
        for k in range(beads):
            mode = modes[step, k]
            for b in range(beads):
                mixed[b] = mixed[b] + table_ref[me_bead * beads + b, first + k] * mode

    charge = charge_ref[...]
    for b in range(beads):
        packs[0, b] = jnp.where(row < 3, mixed[b], jnp.where(row == 3, charge, 0.0))

    def pack_copy(step):
        return pltpu.make_async_remote_copy(
            src_ref=packs.at[0], dst_ref=packs.at[step],
            send_sem=pack_send.at[step], recv_sem=pack_recv.at[step],
            device_id={"dom": lax.rem(me + step, n_dom)}, device_id_type=MESH,
        )

    for step in range(1, half + 1):
        pack_copy(step).start()
    for b in range(beads):
        pos_out[b] = mixed[b][:3]
        speed[b] = pltpu.roll(mixed[b], 4, axis=0)
        pack = packs[0, b]
        centre = jnp.broadcast_to(jnp.mean(pack, axis=1, keepdims=True), tile)
        centres[b] = centre
        pos = scaled(pack, centre)
        near_ops[b] = near_operand(pos)
        moment = moment_parts(pos, charge).T.astype(jnp.bfloat16)
        near_moments[b] = jnp.concatenate((moment, moment), axis=0)
        sums[b] = jnp.zeros((32, tile[1]), jnp.float32)

    def prepare(step):
        for b in range(beads):
            pack = packs[step, b]
            pos = scaled(pack, centres[b])
            lefts[b] = far_operand(pos)
            rights[b] = moment_parts(pos, pack[3:4]).astype(jnp.bfloat16)

    def some_beads(first, with_back):
        square_rows(lefts.at[first], near_ops.at[first], squares.at[0])
        for i in range(group):
            b = first + i
            total = sums[b]
            for start in range(0, tile[1], ROWS):
                weigh_rows(start, squares.at[i], weights.at[i])
                if start == 0 and i + 1 < group:
                    square_rows(lefts.at[b + 1], near_ops.at[b + 1], squares.at[i + 1])
                total += near_sums(start, rights.at[b], weights.at[i])
            sums[b] = total
            if with_back:
                far_sums(near_moments.at[b], weights.at[i], raw_backs.at[b])

    def own_beads(g, unused):
        some_beads(g * group, False)
        return unused

    mine = jnp.where(me < half, 0, part)
    theirs = part - mine

    def back_copy(step):
        span = pl.ds(0, beads)
        return pltpu.make_async_remote_copy(
            src_ref=backs.at[step, span], dst_ref=returned.at[step, span],
            send_sem=back_send.at[step], recv_sem=back_recv.at[step],
            device_id={"dom": lax.rem(me - step + n_dom, n_dom)}, device_id_type=MESH,
        )

    def last_copy(first):
        span = pl.ds(first, part)
        return pltpu.make_async_remote_copy(
            src_ref=backs.at[half, span], dst_ref=returned.at[half, span],
            send_sem=back_send.at[half], recv_sem=back_recv.at[half],
            device_id={"dom": lax.rem(me - half + n_dom, n_dom)}, device_id_type=MESH,
        )

    prepare(0)
    lax.fori_loop(0, part // group, own_beads, 0)

    def one_step(step, unused):
        pack_copy(step).wait_recv()
        prepare(step)
        first = jnp.where(step < half, 0, mine)
        count = jnp.where(step < half, beads // group, part // group)

        def unit(g, inner):
            some_beads(first + g * group, True)
            return inner

        lax.fori_loop(0, count, unit, 0)
        for b in range(beads):
            pack = packs[step, b]
            backs[step, b] = force_of(scaled(pack, centres[b]), pack[3:4], raw_backs[b].T)

        @pl.when(step < half)
        def _():
            back_copy(step).start()

        return unused

    lax.fori_loop(1, half + 1, one_step, 0)
    last_copy(mine).start()
    prepare(0)
    lax.fori_loop(part // group, beads // group, own_beads, 0)

    for b in range(beads):
        pack = packs[0, b]
        pos = scaled(pack, centres[b])
        speed[b] += force_of(pos, pack[3:4], sums[b])

    def collect(step, unused):
        back_copy(step).wait_recv()
        for b in range(beads):
            speed[b] += returned[step, b]
        return unused

    lax.fori_loop(1, half, collect, 0)
    last_copy(theirs).wait_recv()
    for b in range(part):
        speed[theirs + b] += returned[half, theirs + b]
    for b in range(beads):
        vel_out[b] = speed[b, 0:3]

    for step in range(1, n_bead):
        mode_copy(step).wait_send()
    for step in range(1, half + 1):
        pack_copy(step).wait_send()
    for step in range(1, half):
        back_copy(step).wait_send()
    last_copy(mine).wait_send()


def local(mode_pos, mode_vel, charges):
    n_bead, n_dom = lax.axis_size("bead"), lax.axis_size("dom")
    beads, unused, count = mode_pos.shape
    half = n_dom // 2
    total = n_bead * beads
    group = 2 if beads % 4 == 0 else 1
    vmem, smem = pl.BlockSpec(memory_space=pltpu.VMEM), pl.BlockSpec(memory_space=pltpu.SMEM)
    shape = jax.ShapeDtypeStruct(mode_pos.shape, jnp.float32)
    return pl.pallas_call(
        functools.partial(kernel, n_bead, n_dom),
        out_shape=(shape, shape),
        in_specs=[smem, smem, vmem, vmem, vmem],
        out_specs=(vmem, vmem),
        scratch_shapes=[
            pltpu.VMEM((n_bead, beads, 8, count), jnp.float32),
            pltpu.VMEM((half + 1, beads, 8, count), jnp.float32),
            pltpu.VMEM((beads, 8, count), jnp.float32),
            pltpu.VMEM((beads, 8, count), jnp.float32),
            pltpu.VMEM((beads, 48, count), jnp.bfloat16),
            pltpu.VMEM((beads, 2 * count, 32), jnp.bfloat16),
            pltpu.VMEM((beads, 32, count), jnp.float32),
            pltpu.VMEM((half + 1, beads, 8, count), jnp.float32),
            pltpu.VMEM((half + 1, beads, 8, count), jnp.float32),
            pltpu.VMEM((group, count, count), jnp.float32),
            pltpu.VMEM((group, count, 2 * count), jnp.bfloat16),
            pltpu.VMEM((beads, count, 48), jnp.bfloat16),
            pltpu.VMEM((beads, 32, count), jnp.bfloat16),
            pltpu.VMEM((beads, count, 32), jnp.float32),
            pltpu.SemaphoreType.DMA((n_bead,)),
            pltpu.SemaphoreType.DMA((n_bead,)),
            pltpu.SemaphoreType.DMA((half + 1,)),
            pltpu.SemaphoreType.DMA((half + 1,)),
            pltpu.SemaphoreType.DMA((half + 1,)),
            pltpu.SemaphoreType.DMA((half + 1,)),
        ],
        compiler_params=pltpu.CompilerParams(
            collective_id=0, has_side_effects=True, vmem_limit_bytes=48 * 1024 * 1024
        ),
    )(mode_table(total), step_table(total), mode_pos, mode_vel, charges[None])


def solution(mesh):
    placed = (P("bead", None, "dom"), P("bead", None, "dom"), P("dom"))
    return jax.shard_map(
        local,
        mesh=mesh,
        in_specs=placed,
        out_specs=(P("bead", None, "dom"), P("bead", None, "dom")),
        check_vma=False,
    )
```

```python
import functools

import jax
import jax.numpy as jnp
import numpy as np
from jax import lax
from jax.experimental import pallas as pl
from jax.experimental.pallas import tpu as pltpu
from jax.sharding import PartitionSpec as P

KAPPA = 2.0
SOFTEN = 0.09
KICK = 0.3
OMEGA = 7.0
STEP_TIME = 0.1
LOG2E = 1.4426950408889634
ROWS = 256
STRIP = 16
LANES = 256
MESH = pl.DeviceIdType.MESH


def mode_table(beads):
    bead, mode = np.arange(beads)[:, None], np.arange(beads)[None, :]
    angle = 2.0 * np.pi * bead * mode / beads
    wave = np.where(2 * mode < beads, np.cos(angle), np.sin(angle)) * np.sqrt(2.0 / beads)
    edge = np.where(mode == 0, 1.0, np.cos(np.pi * bead)) / np.sqrt(beads)
    return np.where((mode == 0) | (2 * mode == beads), edge, wave).astype(np.float32)


def step_table(beads):
    freq = 2.0 * OMEGA * np.sin(np.pi * np.arange(beads) / beads)
    theta = freq * STEP_TIME
    rate = np.where(freq > 0, np.sin(theta) / np.where(freq > 0, freq, 1.0), STEP_TIME)
    return np.stack((np.cos(theta), rate, -freq * np.sin(theta)), axis=1).astype(np.float32)


def split3(value):
    one = value.astype(jnp.bfloat16).astype(jnp.float32)
    rest = value - one
    two = rest.astype(jnp.bfloat16).astype(jnp.float32)
    return one, two, rest - two


def row_index(shape):
    return lax.broadcasted_iota(jnp.int32, shape, 0)


def scaled(pack, centre):
    return jnp.where(row_index(pack.shape) < 3, KAPPA * (pack - centre), 0.0)


def near_operand(pos):
    row = row_index(pos.shape)
    norm = jnp.sum(pos * pos, axis=0, keepdims=True) + KAPPA * KAPPA * SOFTEN
    one, two, three = split3(jnp.where(row == 3, norm, -2.0 * pos))
    last = row == 3
    groups = (
        one,
        jnp.where(last, two, one),
        jnp.where(last, three, two),
        jnp.where(last, 1.0, two),
        jnp.where(last, 1.0, one),
        jnp.where(last, 1.0, three),
    )
    return jnp.concatenate(groups, axis=0).astype(jnp.bfloat16)


def moment_parts(pos, charge):
    moments = jnp.where(row_index(pos.shape) == 3, charge, pos * charge)
    return jnp.concatenate(split3(moments) + (jnp.zeros_like(pos),), axis=0)


def far_operand(pos):
    last = row_index(pos.shape) == 3
    norm = jnp.sum(pos * pos, axis=0, keepdims=True)
    one, two, three = split3(jnp.where(last, norm, pos))
    first = jnp.where(last, 1.0, one)
    groups = (
        first,
        jnp.where(last, 1.0, two),
        first,
        jnp.where(last, one, two),
        jnp.where(last, two, three),
        jnp.where(last, three, one),
    )
    return jnp.concatenate(groups, axis=0).T.astype(jnp.bfloat16)


def pair_weight(square):
    inverse = lax.rsqrt(square)
    decay = jnp.exp2(square * (inverse * (-LOG2E)))
    return decay * (1.0 + inverse) * (inverse * inverse)


def square_pieces(start, left, near, squares):
    rows = pl.ds(start, ROWS)

    def piece(lanes):
        squares[rows, lanes] = jnp.dot(
            left[rows], near[:, lanes], preferred_element_type=jnp.float32
        )

    return [functools.partial(piece, lanes) for lanes in lane_tiles(squares.shape[1])]


def lane_tiles(count):
    return [pl.ds(lane, LANES) for lane in range(0, count, LANES)]


def weigh_strip(strip, squares, weights):
    count = squares.shape[1]
    weight = pair_weight(squares[strip : strip + STRIP])
    high = weight.astype(jnp.bfloat16)
    low = (weight - high.astype(jnp.float32)).astype(jnp.bfloat16)
    weights[strip : strip + STRIP, :count] = high
    weights[strip : strip + STRIP, count:] = low


def near_pieces(start, right, weights, sums):
    rows, count = pl.ds(start, ROWS), weights.shape[1] // 2

    def piece(lane):
        moment = right[:, rows]
        high = weights[rows, lane : lane + LANES]
        low = weights[rows, count + lane : count + lane + LANES]
        part = jnp.dot(moment, high, preferred_element_type=jnp.float32)
        part += jnp.dot(moment, low, preferred_element_type=jnp.float32)
        sums[:, lane : lane + LANES] += part

    return [functools.partial(piece, lane) for lane in range(0, count, LANES)]


def far_piece(start, near_moment, weights, back):
    rows = pl.ds(start, ROWS)
    back[rows] = jnp.dot(weights[rows], near_moment[...], preferred_element_type=jnp.float32)


def force_of(pos, charge, sums):
    sums = sums[:8] + sums[8:16] + sums[16:24]
    return (4.0 * KICK) * charge * (pos * sums[3:4] - sums)


def kernel(
    n_bead, n_dom, table_ref, step_ref, pos_ref, vel_ref, charge_ref, pos_out, vel_out,
    modes, packs, speed, centres, near_ops, near_moments, sums, backs, returned, squares, weights,
    lefts, rights, raw_backs, mode_send, mode_recv, pack_send, pack_recv, back_send, back_recv,
):
    me_bead, me = lax.axis_index("bead"), lax.axis_index("dom")
    beads, half = pos_ref.shape[0], n_dom // 2
    part = beads // 2
    group = squares.shape[0]
    tile = (8, pos_ref.shape[2])
    row = row_index(tile)

    barrier = pltpu.get_barrier_semaphore()
    for step in range(1, n_bead):
        pl.semaphore_signal(
            barrier, inc=1, device_id={"bead": lax.rem(me_bead + step, n_bead)}, device_id_type=MESH
        )
    for step in range(1, n_dom):
        pl.semaphore_signal(
            barrier, inc=1, device_id={"dom": lax.rem(me + step, n_dom)}, device_id_type=MESH
        )

    for k in range(beads):
        mode = me_bead * beads + k
        old_pos, old_vel = pos_ref[k], vel_ref[k]
        modes[0, k] = jnp.zeros(tile, jnp.float32)
        modes[0, k, 0:3] = step_ref[mode, 0] * old_pos + step_ref[mode, 1] * old_vel
        modes[0, k, 4:7] = step_ref[mode, 2] * old_pos + step_ref[mode, 0] * old_vel
    pl.semaphore_wait(barrier, n_bead + n_dom - 2)

    def mode_copy(step):
        return pltpu.make_async_remote_copy(
            src_ref=modes.at[0], dst_ref=modes.at[step],
            send_sem=mode_send.at[step], recv_sem=mode_recv.at[step],
            device_id={"bead": lax.rem(me_bead + step, n_bead)}, device_id_type=MESH,
        )

    for step in range(1, n_bead):
        mode_copy(step).start()
    mixed = [jnp.zeros(tile, jnp.float32) for b in range(beads)]
    for step in range(n_bead):
        if step:
            mode_copy(step).wait_recv()
        first = lax.rem(me_bead - step + n_bead, n_bead) * beads
        for k in range(beads):
            mode = modes[step, k]
            for b in range(beads):
                mixed[b] = mixed[b] + table_ref[me_bead * beads + b, first + k] * mode

    charge = charge_ref[...]
    for b in range(beads):
        packs[0, b] = jnp.where(row < 3, mixed[b], jnp.where(row == 3, charge, 0.0))

    def pack_copy(step):
        return pltpu.make_async_remote_copy(
            src_ref=packs.at[0], dst_ref=packs.at[step],
            send_sem=pack_send.at[step], recv_sem=pack_recv.at[step],
            device_id={"dom": lax.rem(me + step, n_dom)}, device_id_type=MESH,
        )

    for step in range(1, half + 1):
        pack_copy(step).start()
    for b in range(beads):
        pos_out[b] = mixed[b][:3]
        speed[b] = pltpu.roll(mixed[b], 4, axis=0)
        pack = packs[0, b]
        centre = jnp.broadcast_to(jnp.mean(pack, axis=1, keepdims=True), tile)
        centres[b] = centre
        pos = scaled(pack, centre)
        near_ops[b] = near_operand(pos)
        moment = moment_parts(pos, charge).T.astype(jnp.bfloat16)
        near_moments[b] = jnp.concatenate((moment, moment), axis=0)
        sums[b] = jnp.zeros((32, tile[1]), jnp.float32)

    def prepare(step):
        for b in range(beads):
            pack = packs[step, b]
            pos = scaled(pack, centres[b])
            lefts[b] = far_operand(pos)
            rights[b] = moment_parts(pos, pack[3:4]).astype(jnp.bfloat16)

    def some_beads(first, with_back):
        chunks = [(i, start) for i in range(group) for start in range(0, tile[1], ROWS)]

        def before(turn):
            i, start = chunks[turn]
            b = first + i
            return square_pieces(start, lefts.at[b], near_ops.at[b], squares.at[i])

        def after(turn):
            i, start = chunks[turn]
            b = first + i
            pieces = near_pieces(start, rights.at[b], weights.at[i], sums.at[b])
            if with_back:
                one = functools.partial(
                    far_piece, start, near_moments.at[b], weights.at[i], raw_backs.at[b]
                )
                pieces.insert(1, one)
            return pieces

        for piece in before(0):
            piece()
        for turn, (i, start) in enumerate(chunks):
            pieces = after(turn - 1) if turn else []
            pieces += before(turn + 1) if turn + 1 < len(chunks) else []
            strips = list(range(start, start + ROWS, STRIP))
            for n, strip in enumerate(strips):
                weigh_strip(strip, squares.at[i], weights.at[i])
                if pieces and n % 2 == 0:
                    pieces.pop(0)()
            for piece in pieces:
                piece()
        for piece in after(len(chunks) - 1):
            piece()

    def own_beads(g, unused):
        some_beads(g * group, False)
        return unused

    mine = jnp.where(me < half, 0, part)
    theirs = part - mine

    def back_copy(step):
        span = pl.ds(0, beads)
        return pltpu.make_async_remote_copy(
            src_ref=backs.at[step, span], dst_ref=returned.at[step, span],
            send_sem=back_send.at[step], recv_sem=back_recv.at[step],
            device_id={"dom": lax.rem(me - step + n_dom, n_dom)}, device_id_type=MESH,
        )

    def last_copy(first):
        span = pl.ds(first, part)
        return pltpu.make_async_remote_copy(
            src_ref=backs.at[half, span], dst_ref=returned.at[half, span],
            send_sem=back_send.at[half], recv_sem=back_recv.at[half],
            device_id={"dom": lax.rem(me - half + n_dom, n_dom)}, device_id_type=MESH,
        )

    prepare(0)
    lax.fori_loop(0, part // group, own_beads, 0)

    def one_step(step, unused):
        pack_copy(step).wait_recv()
        prepare(step)
        first = jnp.where(step < half, 0, mine)
        count = jnp.where(step < half, beads // group, part // group)

        def unit(g, inner):
            some_beads(first + g * group, True)
            return inner

        lax.fori_loop(0, count, unit, 0)
        for b in range(beads):
            pack = packs[step, b]
            backs[step, b] = force_of(scaled(pack, centres[b]), pack[3:4], raw_backs[b].T)

        @pl.when(step < half)
        def _():
            back_copy(step).start()

        return unused

    lax.fori_loop(1, half + 1, one_step, 0)
    last_copy(mine).start()
    prepare(0)
    lax.fori_loop(part // group, beads // group, own_beads, 0)

    for b in range(beads):
        pack = packs[0, b]
        pos = scaled(pack, centres[b])
        speed[b] += force_of(pos, pack[3:4], sums[b])

    def collect(step, unused):
        back_copy(step).wait_recv()
        for b in range(beads):
            speed[b] += returned[step, b]
        return unused

    lax.fori_loop(1, half, collect, 0)
    last_copy(theirs).wait_recv()
    for b in range(part):
        speed[theirs + b] += returned[half, theirs + b]
    for b in range(beads):
        vel_out[b] = speed[b, 0:3]

    for step in range(1, n_bead):
        mode_copy(step).wait_send()
    for step in range(1, half + 1):
        pack_copy(step).wait_send()
    for step in range(1, half):
        back_copy(step).wait_send()
    last_copy(mine).wait_send()


def local(mode_pos, mode_vel, charges):
    n_bead, n_dom = lax.axis_size("bead"), lax.axis_size("dom")
    beads, unused, count = mode_pos.shape
    half = n_dom // 2
    total = n_bead * beads
    group = 2 if beads % 4 == 0 else 1
    vmem, smem = pl.BlockSpec(memory_space=pltpu.VMEM), pl.BlockSpec(memory_space=pltpu.SMEM)
    shape = jax.ShapeDtypeStruct(mode_pos.shape, jnp.float32)
    return pl.pallas_call(
        functools.partial(kernel, n_bead, n_dom),
        out_shape=(shape, shape),
        in_specs=[smem, smem, vmem, vmem, vmem],
        out_specs=(vmem, vmem),
        scratch_shapes=[
            pltpu.VMEM((n_bead, beads, 8, count), jnp.float32),
            pltpu.VMEM((half + 1, beads, 8, count), jnp.float32),
            pltpu.VMEM((beads, 8, count), jnp.float32),
            pltpu.VMEM((beads, 8, count), jnp.float32),
            pltpu.VMEM((beads, 48, count), jnp.bfloat16),
            pltpu.VMEM((beads, 2 * count, 32), jnp.bfloat16),
            pltpu.VMEM((beads, 32, count), jnp.float32),
            pltpu.VMEM((half + 1, beads, 8, count), jnp.float32),
            pltpu.VMEM((half + 1, beads, 8, count), jnp.float32),
            pltpu.VMEM((group, count, count), jnp.float32),
            pltpu.VMEM((group, count, 2 * count), jnp.bfloat16),
            pltpu.VMEM((beads, count, 48), jnp.bfloat16),
            pltpu.VMEM((beads, 32, count), jnp.bfloat16),
            pltpu.VMEM((beads, count, 32), jnp.float32),
            pltpu.SemaphoreType.DMA((n_bead,)),
            pltpu.SemaphoreType.DMA((n_bead,)),
            pltpu.SemaphoreType.DMA((half + 1,)),
            pltpu.SemaphoreType.DMA((half + 1,)),
            pltpu.SemaphoreType.DMA((half + 1,)),
            pltpu.SemaphoreType.DMA((half + 1,)),
        ],
        compiler_params=pltpu.CompilerParams(
            collective_id=0, has_side_effects=True, vmem_limit_bytes=48 * 1024 * 1024
        ),
    )(mode_table(total), step_table(total), mode_pos, mode_vel, charges[None])


def solution(mesh):
    placed = (P("bead", None, "dom"), P("bead", None, "dom"), P("dom"))
    return jax.shard_map(
        local,
        mesh=mesh,
        in_specs=placed,
        out_specs=(P("bead", None, "dom"), P("bead", None, "dom")),
        check_vma=False,
    )
```

```python
import functools

import jax
import jax.numpy as jnp
import numpy as np
from jax import lax
from jax.experimental import pallas as pl
from jax.experimental.pallas import tpu as pltpu
from jax.sharding import PartitionSpec as P

KAPPA = 2.0
SOFTEN = 0.09
KICK = 0.3
OMEGA = 7.0
STEP_TIME = 0.1
LOG2E = 1.4426950408889634
ROWS = 256
STRIP = 16
LANES = 256
MESH = pl.DeviceIdType.MESH


def mode_table(beads):
    bead, mode = np.arange(beads)[:, None], np.arange(beads)[None, :]
    angle = 2.0 * np.pi * bead * mode / beads
    wave = np.where(2 * mode < beads, np.cos(angle), np.sin(angle)) * np.sqrt(2.0 / beads)
    edge = np.where(mode == 0, 1.0, np.cos(np.pi * bead)) / np.sqrt(beads)
    return np.where((mode == 0) | (2 * mode == beads), edge, wave).astype(np.float32)


def step_table(beads):
    freq = 2.0 * OMEGA * np.sin(np.pi * np.arange(beads) / beads)
    theta = freq * STEP_TIME
    rate = np.where(freq > 0, np.sin(theta) / np.where(freq > 0, freq, 1.0), STEP_TIME)
    return np.stack((np.cos(theta), rate, -freq * np.sin(theta)), axis=1).astype(np.float32)


def split3(value):
    one = value.astype(jnp.bfloat16).astype(jnp.float32)
    rest = value - one
    two = rest.astype(jnp.bfloat16).astype(jnp.float32)
    return one, two, rest - two


def row_index(shape):
    return lax.broadcasted_iota(jnp.int32, shape, 0)


def scaled(pack, centre):
    return jnp.where(row_index(pack.shape) < 3, KAPPA * (pack - centre), 0.0)


def near_operand(pos):
    row = row_index(pos.shape)
    norm = jnp.sum(pos * pos, axis=0, keepdims=True) + KAPPA * KAPPA * SOFTEN
    one, two, three = split3(jnp.where(row == 3, norm, -2.0 * pos))
    last = row == 3
    groups = (
        one,
        jnp.where(last, two, one),
        jnp.where(last, three, two),
        jnp.where(last, 1.0, two),
        jnp.where(last, 1.0, one),
        jnp.where(last, 1.0, three),
    )
    return jnp.concatenate(groups, axis=0).astype(jnp.bfloat16)


def moment_parts(pos, charge):
    moments = jnp.where(row_index(pos.shape) == 3, charge, pos * charge)
    return jnp.concatenate(split3(moments) + (jnp.zeros_like(pos),), axis=0)


def far_operand(pos):
    last = row_index(pos.shape) == 3
    norm = jnp.sum(pos * pos, axis=0, keepdims=True)
    one, two, three = split3(jnp.where(last, norm, pos))
    first = jnp.where(last, 1.0, one)
    groups = (
        first,
        jnp.where(last, 1.0, two),
        first,
        jnp.where(last, one, two),
        jnp.where(last, two, three),
        jnp.where(last, three, one),
    )
    return jnp.concatenate(groups, axis=0).T.astype(jnp.bfloat16)


def pair_weight(square):
    inverse = lax.rsqrt(square)
    decay = jnp.exp2(square * (inverse * (-LOG2E)))
    return decay * (1.0 + inverse) * (inverse * inverse)


def square_pieces(start, left, near, squares):
    rows = pl.ds(start, ROWS)

    def piece(lanes):
        squares[rows, lanes] = jnp.dot(
            left[rows], near[:, lanes], preferred_element_type=jnp.float32
        )

    return [functools.partial(piece, lanes) for lanes in lane_tiles(squares.shape[1])]


def lane_tiles(count):
    return [pl.ds(lane, LANES) for lane in range(0, count, LANES)]


def weigh_strip(strip, squares, weights):
    count = squares.shape[1]
    weight = pair_weight(squares[strip : strip + STRIP])
    high = weight.astype(jnp.bfloat16)
    low = (weight - high.astype(jnp.float32)).astype(jnp.bfloat16)
    weights[strip : strip + STRIP, :count] = high
    weights[strip : strip + STRIP, count:] = low


def near_pieces(start, right, weights, sums):
    rows, count = pl.ds(start, ROWS), weights.shape[1] // 2

    def piece(lane):
        moment = right[:, rows]
        high = weights[rows, lane : lane + LANES]
        low = weights[rows, count + lane : count + lane + LANES]
        part = jnp.dot(moment, high, preferred_element_type=jnp.float32)
        part += jnp.dot(moment, low, preferred_element_type=jnp.float32)
        sums[:, lane : lane + LANES] += part

    return [functools.partial(piece, lane) for lane in range(0, count, LANES)]


def far_piece(start, near_moment, weights, back):
    rows = pl.ds(start, ROWS)
    back[:, rows] = lax.dot_general(
        near_moment[...], weights[rows], (((1,), (1,)), ((), ())),
        preferred_element_type=jnp.float32,
    )


def force_of(pos, charge, sums):
    sums = sums[:8] + sums[8:16] + sums[16:24]
    return (4.0 * KICK) * charge * (pos * sums[3:4] - sums)


def kernel(
    n_bead, n_dom, table_ref, step_ref, pos_ref, vel_ref, charge_ref, pos_out, vel_out,
    modes, packs, speed, centres, near_ops, near_moments, sums, backs, returned, squares, weights,
    lefts, rights, raw_backs, mode_send, mode_recv, pack_send, pack_recv, back_send, back_recv,
):
    me_bead, me = lax.axis_index("bead"), lax.axis_index("dom")
    beads, half = pos_ref.shape[0], n_dom // 2
    part = beads // 2
    group = squares.shape[0]
    tile = (8, pos_ref.shape[2])
    row = row_index(tile)

    barrier = pltpu.get_barrier_semaphore()
    for step in range(1, n_bead):
        pl.semaphore_signal(
            barrier, inc=1, device_id={"bead": lax.rem(me_bead + step, n_bead)}, device_id_type=MESH
        )
    for step in range(1, n_dom):
        pl.semaphore_signal(
            barrier, inc=1, device_id={"dom": lax.rem(me + step, n_dom)}, device_id_type=MESH
        )

    for k in range(beads):
        mode = me_bead * beads + k
        old_pos, old_vel = pos_ref[k], vel_ref[k]
        modes[0, k] = jnp.zeros(tile, jnp.float32)
        modes[0, k, 0:3] = step_ref[mode, 0] * old_pos + step_ref[mode, 1] * old_vel
        modes[0, k, 4:7] = step_ref[mode, 2] * old_pos + step_ref[mode, 0] * old_vel
    pl.semaphore_wait(barrier, n_bead + n_dom - 2)

    def mode_copy(step):
        return pltpu.make_async_remote_copy(
            src_ref=modes.at[0], dst_ref=modes.at[step],
            send_sem=mode_send.at[step], recv_sem=mode_recv.at[step],
            device_id={"bead": lax.rem(me_bead + step, n_bead)}, device_id_type=MESH,
        )

    for step in range(1, n_bead):
        mode_copy(step).start()
    mixed = [jnp.zeros(tile, jnp.float32) for b in range(beads)]
    for step in range(n_bead):
        if step:
            mode_copy(step).wait_recv()
        first = lax.rem(me_bead - step + n_bead, n_bead) * beads
        for k in range(beads):
            mode = modes[step, k]
            for b in range(beads):
                mixed[b] = mixed[b] + table_ref[me_bead * beads + b, first + k] * mode

    charge = charge_ref[...].reshape(1, tile[1])
    for b in range(beads):
        packs[0, b] = jnp.where(row < 3, mixed[b], jnp.where(row == 3, charge, 0.0))

    def pack_copy(step):
        return pltpu.make_async_remote_copy(
            src_ref=packs.at[0], dst_ref=packs.at[step],
            send_sem=pack_send.at[step], recv_sem=pack_recv.at[step],
            device_id={"dom": lax.rem(me + step, n_dom)}, device_id_type=MESH,
        )

    for step in range(1, half + 1):
        pack_copy(step).start()
    for b in range(beads):
        pos_out[b] = mixed[b][:3]
        speed[b] = pltpu.roll(mixed[b], 4, axis=0)
        pack = packs[0, b]
        centre = jnp.broadcast_to(jnp.mean(pack, axis=1, keepdims=True), tile)
        centres[b] = centre
        pos = scaled(pack, centre)
        near_ops[b] = near_operand(pos)
        moment = moment_parts(pos, charge).astype(jnp.bfloat16)
        near_moments[b] = jnp.concatenate((moment, moment), axis=1)
        sums[b] = jnp.zeros((32, tile[1]), jnp.float32)

    def prepare(step):
        for b in range(beads):
            pack = packs[step, b]
            pos = scaled(pack, centres[b])
            lefts[b] = far_operand(pos)
            rights[b] = moment_parts(pos, pack[3:4]).astype(jnp.bfloat16)

    def some_beads(first, with_back):
        chunks = [(i, start) for i in range(group) for start in range(0, tile[1], ROWS)]

        def before(turn):
            i, start = chunks[turn]
            b = first + i
            return square_pieces(start, lefts.at[b], near_ops.at[b], squares.at[i])

        def after(turn):
            i, start = chunks[turn]
            b = first + i
            pieces = near_pieces(start, rights.at[b], weights.at[i], sums.at[b])
            if with_back:
                one = functools.partial(
                    far_piece, start, near_moments.at[b], weights.at[i], raw_backs.at[b]
                )
                pieces.insert(1, one)
            return pieces

        for piece in before(0):
            piece()
        for turn, (i, start) in enumerate(chunks):
            pieces = after(turn - 1) if turn else []
            pieces += before(turn + 1) if turn + 1 < len(chunks) else []
            strips = list(range(start, start + ROWS, STRIP))
            for n, strip in enumerate(strips):
                weigh_strip(strip, squares.at[i], weights.at[i])
                if pieces and n % 2 == 0:
                    pieces.pop(0)()
            for piece in pieces:
                piece()
        for piece in after(len(chunks) - 1):
            piece()

    def own_beads(g, unused):
        some_beads(g * group, False)
        return unused

    mine = jnp.where(me < half, 0, part)
    theirs = part - mine

    def back_copy(step):
        span = pl.ds(0, beads)
        return pltpu.make_async_remote_copy(
            src_ref=backs.at[step, span], dst_ref=returned.at[step, span],
            send_sem=back_send.at[step], recv_sem=back_recv.at[step],
            device_id={"dom": lax.rem(me - step + n_dom, n_dom)}, device_id_type=MESH,
        )

    def last_copy(first):
        span = pl.ds(first, part)
        return pltpu.make_async_remote_copy(
            src_ref=backs.at[half, span], dst_ref=returned.at[half, span],
            send_sem=back_send.at[half], recv_sem=back_recv.at[half],
            device_id={"dom": lax.rem(me - half + n_dom, n_dom)}, device_id_type=MESH,
        )

    prepare(0)
    lax.fori_loop(0, part // group, own_beads, 0)

    def one_step(step, unused):
        pack_copy(step).wait_recv()
        prepare(step)
        first = jnp.where(step < half, 0, mine)
        count = jnp.where(step < half, beads // group, part // group)

        def unit(g, inner):
            some_beads(first + g * group, True)
            return inner

        lax.fori_loop(0, count, unit, 0)
        for b in range(beads):
            pack = packs[step, b]
            backs[step, b] = force_of(scaled(pack, centres[b]), pack[3:4], raw_backs[b])

        @pl.when(step < half)
        def _():
            back_copy(step).start()

        return unused

    lax.fori_loop(1, half + 1, one_step, 0)
    last_copy(mine).start()
    prepare(0)
    lax.fori_loop(part // group, beads // group, own_beads, 0)

    for b in range(beads):
        pack = packs[0, b]
        pos = scaled(pack, centres[b])
        speed[b] += force_of(pos, pack[3:4], sums[b])

    def collect(step, unused):
        back_copy(step).wait_recv()
        for b in range(beads):
            speed[b] += returned[step, b]
        return unused

    lax.fori_loop(1, half, collect, 0)
    last_copy(theirs).wait_recv()
    for b in range(part):
        speed[theirs + b] += returned[half, theirs + b]
    for b in range(beads):
        vel_out[b] = speed[b, 0:3]

    for step in range(1, n_bead):
        mode_copy(step).wait_send()
    for step in range(1, half + 1):
        pack_copy(step).wait_send()
    for step in range(1, half):
        back_copy(step).wait_send()
    last_copy(mine).wait_send()


def local(mode_pos, mode_vel, charges):
    n_bead, n_dom = lax.axis_size("bead"), lax.axis_size("dom")
    beads, unused, count = mode_pos.shape
    half = n_dom // 2
    total = n_bead * beads
    group = 2 if beads % 4 == 0 else 1
    vmem, smem = pl.BlockSpec(memory_space=pltpu.VMEM), pl.BlockSpec(memory_space=pltpu.SMEM)
    shape = jax.ShapeDtypeStruct(mode_pos.shape, jnp.float32)
    return pl.pallas_call(
        functools.partial(kernel, n_bead, n_dom),
        out_shape=(shape, shape),
        in_specs=[smem, smem, vmem, vmem, vmem],
        out_specs=(vmem, vmem),
        scratch_shapes=[
            pltpu.VMEM((n_bead, beads, 8, count), jnp.float32),
            pltpu.VMEM((half + 1, beads, 8, count), jnp.float32),
            pltpu.VMEM((beads, 8, count), jnp.float32),
            pltpu.VMEM((beads, 8, count), jnp.float32),
            pltpu.VMEM((beads, 48, count), jnp.bfloat16),
            pltpu.VMEM((beads, 32, 2 * count), jnp.bfloat16),
            pltpu.VMEM((beads, 32, count), jnp.float32),
            pltpu.VMEM((half + 1, beads, 8, count), jnp.float32),
            pltpu.VMEM((half + 1, beads, 8, count), jnp.float32),
            pltpu.VMEM((group, count, count), jnp.float32),
            pltpu.VMEM((group, count, 2 * count), jnp.bfloat16),
            pltpu.VMEM((beads, count, 48), jnp.bfloat16),
            pltpu.VMEM((beads, 32, count), jnp.bfloat16),
            pltpu.VMEM((beads, 32, count), jnp.float32),
            pltpu.SemaphoreType.DMA((n_bead,)),
            pltpu.SemaphoreType.DMA((n_bead,)),
            pltpu.SemaphoreType.DMA((half + 1,)),
            pltpu.SemaphoreType.DMA((half + 1,)),
            pltpu.SemaphoreType.DMA((half + 1,)),
            pltpu.SemaphoreType.DMA((half + 1,)),
        ],
        compiler_params=pltpu.CompilerParams(
            collective_id=0, has_side_effects=True, vmem_limit_bytes=48 * 1024 * 1024
        ),
    )(mode_table(total), step_table(total), mode_pos, mode_vel, charges)


def solution(mesh):
    placed = (P("bead", None, "dom"), P("bead", None, "dom"), P("dom"))
    return jax.shard_map(
        local,
        mesh=mesh,
        in_specs=placed,
        out_specs=(P("bead", None, "dom"), P("bead", None, "dom")),
        check_vma=False,
    )
```

```python
import functools

import jax
import jax.numpy as jnp
import numpy as np
from jax import lax
from jax.experimental import pallas as pl
from jax.experimental.pallas import tpu as pltpu
from jax.sharding import PartitionSpec as P

KAPPA = 2.0
SOFTEN = 0.09
KICK = 0.3
OMEGA = 7.0
STEP_TIME = 0.1
LOG2E = 1.4426950408889634
ROWS = 256
STRIP = 16
LANES = 256
MESH = pl.DeviceIdType.MESH


def mode_table(beads):
    bead, mode = np.arange(beads)[:, None], np.arange(beads)[None, :]
    angle = 2.0 * np.pi * bead * mode / beads
    wave = np.where(2 * mode < beads, np.cos(angle), np.sin(angle)) * np.sqrt(2.0 / beads)
    edge = np.where(mode == 0, 1.0, np.cos(np.pi * bead)) / np.sqrt(beads)
    return np.where((mode == 0) | (2 * mode == beads), edge, wave).astype(np.float32)


def step_table(beads):
    freq = 2.0 * OMEGA * np.sin(np.pi * np.arange(beads) / beads)
    theta = freq * STEP_TIME
    rate = np.where(freq > 0, np.sin(theta) / np.where(freq > 0, freq, 1.0), STEP_TIME)
    return np.stack((np.cos(theta), rate, -freq * np.sin(theta)), axis=1).astype(np.float32)


def split3(value):
    one = value.astype(jnp.bfloat16).astype(jnp.float32)
    rest = value - one
    two = rest.astype(jnp.bfloat16).astype(jnp.float32)
    return one, two, rest - two


def row_index(shape):
    return lax.broadcasted_iota(jnp.int32, shape, 0)


def scaled(pack, centre):
    return jnp.where(row_index(pack.shape) < 3, KAPPA * (pack - centre), 0.0)


def near_operand(pos):
    row = row_index(pos.shape)
    norm = jnp.sum(pos * pos, axis=0, keepdims=True) + KAPPA * KAPPA * SOFTEN
    one, two, three = split3(jnp.where(row == 3, norm, -2.0 * pos))
    last = row == 3
    groups = (
        one,
        jnp.where(last, two, one),
        jnp.where(last, three, two),
        jnp.where(last, 1.0, two),
        jnp.where(last, 1.0, one),
        jnp.where(last, 1.0, three),
    )
    return jnp.concatenate(groups, axis=0).astype(jnp.bfloat16)


def moment_parts(pos, charge):
    moments = jnp.where(row_index(pos.shape) == 3, charge, pos * charge)
    return jnp.concatenate(split3(moments) + (jnp.zeros_like(pos),), axis=0)


def far_operand(pos):
    last = row_index(pos.shape) == 3
    norm = jnp.sum(pos * pos, axis=0, keepdims=True)
    one, two, three = split3(jnp.where(last, norm, pos))
    first = jnp.where(last, 1.0, one)
    groups = (
        first,
        jnp.where(last, 1.0, two),
        first,
        jnp.where(last, one, two),
        jnp.where(last, two, three),
        jnp.where(last, three, one),
    )
    return jnp.concatenate(groups, axis=0).T.astype(jnp.bfloat16)


def pair_weight(square):
    inverse = lax.rsqrt(square)
    decay = jnp.exp2(square * (inverse * (-LOG2E)))
    return decay * (1.0 + inverse) * (inverse * inverse)


def square_pieces(start, left, near, squares):
    rows = pl.ds(start, ROWS)

    def piece(lanes):
        squares[rows, lanes] = jnp.dot(
            left[rows], near[:, lanes], preferred_element_type=jnp.float32
        )

    return [functools.partial(piece, lanes) for lanes in lane_tiles(squares.shape[1])]


def lane_tiles(count):
    return [pl.ds(lane, LANES) for lane in range(0, count, LANES)]


def weigh_strip(strip, squares, weights):
    count = squares.shape[1]
    weight = pair_weight(squares[strip : strip + STRIP])
    high = weight.astype(jnp.bfloat16)
    low = (weight - high.astype(jnp.float32)).astype(jnp.bfloat16)
    weights[strip : strip + STRIP, :count] = high
    weights[strip : strip + STRIP, count:] = low


def near_pieces(start, right, weights, sums):
    rows, count = pl.ds(start, ROWS), weights.shape[1] // 2

    def piece(lane):
        moment = right[:, rows]
        high = weights[rows, lane : lane + LANES]
        low = weights[rows, count + lane : count + lane + LANES]
        part = jnp.dot(moment, high, preferred_element_type=jnp.float32)
        part += jnp.dot(moment, low, preferred_element_type=jnp.float32)
        sums[:, lane : lane + LANES] += part

    return [functools.partial(piece, lane) for lane in range(0, count, LANES)]


def far_pieces(start, near_moment, weights, back):
    rows, count = pl.ds(start, ROWS), weights.shape[1] // 2

    def piece(first):
        part = lax.dot_general(
            near_moment[...], weights[rows, first : first + count], (((1,), (1,)), ((), ())),
            preferred_element_type=jnp.float32,
        )
        back[:, rows] = part if first == 0 else back[:, rows] + part

    return [functools.partial(piece, first) for first in (0, count)]


def force_of(pos, charge, sums):
    sums = sums[:8] + sums[8:16] + sums[16:24]
    return (4.0 * KICK) * charge * (pos * sums[3:4] - sums)


def kernel(
    n_bead, n_dom, table_ref, step_ref, pos_ref, vel_ref, charge_ref, pos_out, vel_out,
    modes, packs, speed, centres, near_ops, near_moments, sums, backs, returned, squares, weights,
    lefts, rights, raw_backs, mode_send, mode_recv, pack_send, pack_recv, back_send, back_recv,
):
    me_bead, me = lax.axis_index("bead"), lax.axis_index("dom")
    beads, half = pos_ref.shape[0], n_dom // 2
    part = beads // 2
    group = squares.shape[0]
    tile = (8, pos_ref.shape[2])
    row = row_index(tile)

    barrier = pltpu.get_barrier_semaphore()
    for step in range(1, n_bead):
        pl.semaphore_signal(
            barrier, inc=1, device_id={"bead": lax.rem(me_bead + step, n_bead)}, device_id_type=MESH
        )
    for step in range(1, n_dom):
        pl.semaphore_signal(
            barrier, inc=1, device_id={"dom": lax.rem(me + step, n_dom)}, device_id_type=MESH
        )

    for k in range(beads):
        mode = me_bead * beads + k
        old_pos, old_vel = pos_ref[k], vel_ref[k]
        modes[0, k] = jnp.zeros(tile, jnp.float32)
        modes[0, k, 0:3] = step_ref[mode, 0] * old_pos + step_ref[mode, 1] * old_vel
        modes[0, k, 4:7] = step_ref[mode, 2] * old_pos + step_ref[mode, 0] * old_vel
    pl.semaphore_wait(barrier, n_bead + n_dom - 2)

    def mode_copy(step):
        return pltpu.make_async_remote_copy(
            src_ref=modes.at[0], dst_ref=modes.at[step],
            send_sem=mode_send.at[step], recv_sem=mode_recv.at[step],
            device_id={"bead": lax.rem(me_bead + step, n_bead)}, device_id_type=MESH,
        )

    for step in range(1, n_bead):
        mode_copy(step).start()
    mixed = [jnp.zeros(tile, jnp.float32) for b in range(beads)]
    for step in range(n_bead):
        if step:
            mode_copy(step).wait_recv()
        first = lax.rem(me_bead - step + n_bead, n_bead) * beads
        for k in range(beads):
            mode = modes[step, k]
            for b in range(beads):
                mixed[b] = mixed[b] + table_ref[me_bead * beads + b, first + k] * mode

    charge = charge_ref[...].reshape(1, tile[1])
    for b in range(beads):
        packs[0, b] = jnp.where(row < 3, mixed[b], jnp.where(row == 3, charge, 0.0))

    def pack_copy(step):
        return pltpu.make_async_remote_copy(
            src_ref=packs.at[0], dst_ref=packs.at[step],
            send_sem=pack_send.at[step], recv_sem=pack_recv.at[step],
            device_id={"dom": lax.rem(me + step, n_dom)}, device_id_type=MESH,
        )

    for step in range(1, half + 1):
        pack_copy(step).start()
    for b in range(beads):
        pos_out[b] = mixed[b][:3]
        speed[b] = pltpu.roll(mixed[b], 4, axis=0)
        pack = packs[0, b]
        centre = jnp.broadcast_to(jnp.mean(pack, axis=1, keepdims=True), tile)
        centres[b] = centre
        pos = scaled(pack, centre)
        near_ops[b] = near_operand(pos)
        near_moments[b] = moment_parts(pos, charge).astype(jnp.bfloat16)
        sums[b] = jnp.zeros((32, tile[1]), jnp.float32)

    def prepare(step):
        for b in range(beads):
            pack = packs[step, b]
            pos = scaled(pack, centres[b])
            lefts[b] = far_operand(pos)
            rights[b] = moment_parts(pos, pack[3:4]).astype(jnp.bfloat16)

    def some_beads(first, with_back):
        chunks = [(i, start) for i in range(group) for start in range(0, tile[1], ROWS)]

        def before(turn):
            i, start = chunks[turn]
            b = first + i
            return square_pieces(start, lefts.at[b], near_ops.at[b], squares.at[i])

        def after(turn):
            i, start = chunks[turn]
            b = first + i
            pieces = near_pieces(start, rights.at[b], weights.at[i], sums.at[b])
            if with_back:
                ones = far_pieces(start, near_moments.at[b], weights.at[i], raw_backs.at[b])
                pieces = [pieces[0], ones[0], pieces[1], ones[1], *pieces[2:]]
            return pieces

        for piece in before(0):
            piece()
        for turn, (i, start) in enumerate(chunks):
            pieces = after(turn - 1) if turn else []
            pieces += before(turn + 1) if turn + 1 < len(chunks) else []
            strips = list(range(start, start + ROWS, STRIP))
            for n, strip in enumerate(strips):
                weigh_strip(strip, squares.at[i], weights.at[i])
                if pieces and n % 2 == 0:
                    pieces.pop(0)()
            for piece in pieces:
                piece()
        for piece in after(len(chunks) - 1):
            piece()

    def own_beads(g, unused):
        some_beads(g * group, False)
        return unused

    mine = jnp.where(me < half, 0, part)
    theirs = part - mine

    def back_copy(step):
        span = pl.ds(0, beads)
        return pltpu.make_async_remote_copy(
            src_ref=backs.at[step, span], dst_ref=returned.at[step, span],
            send_sem=back_send.at[step], recv_sem=back_recv.at[step],
            device_id={"dom": lax.rem(me - step + n_dom, n_dom)}, device_id_type=MESH,
        )

    def last_copy(first):
        span = pl.ds(first, part)
        return pltpu.make_async_remote_copy(
            src_ref=backs.at[half, span], dst_ref=returned.at[half, span],
            send_sem=back_send.at[half], recv_sem=back_recv.at[half],
            device_id={"dom": lax.rem(me - half + n_dom, n_dom)}, device_id_type=MESH,
        )

    prepare(0)
    lax.fori_loop(0, part // group, own_beads, 0)

    def one_step(step, unused):
        pack_copy(step).wait_recv()
        prepare(step)
        first = jnp.where(step < half, 0, mine)
        count = jnp.where(step < half, beads // group, part // group)

        def unit(g, inner):
            some_beads(first + g * group, True)
            return inner

        lax.fori_loop(0, count, unit, 0)
        for b in range(beads):
            pack = packs[step, b]
            backs[step, b] = force_of(scaled(pack, centres[b]), pack[3:4], raw_backs[b])

        @pl.when(step < half)
        def _():
            back_copy(step).start()

        return unused

    lax.fori_loop(1, half + 1, one_step, 0)
    last_copy(mine).start()
    prepare(0)
    lax.fori_loop(part // group, beads // group, own_beads, 0)

    for b in range(beads):
        pack = packs[0, b]
        pos = scaled(pack, centres[b])
        speed[b] += force_of(pos, pack[3:4], sums[b])

    def collect(step, unused):
        back_copy(step).wait_recv()
        for b in range(beads):
            speed[b] += returned[step, b]
        return unused

    lax.fori_loop(1, half, collect, 0)
    last_copy(theirs).wait_recv()
    for b in range(part):
        speed[theirs + b] += returned[half, theirs + b]
    for b in range(beads):
        vel_out[b] = speed[b, 0:3]

    for step in range(1, n_bead):
        mode_copy(step).wait_send()
    for step in range(1, half + 1):
        pack_copy(step).wait_send()
    for step in range(1, half):
        back_copy(step).wait_send()
    last_copy(mine).wait_send()


def local(mode_pos, mode_vel, charges):
    n_bead, n_dom = lax.axis_size("bead"), lax.axis_size("dom")
    beads, unused, count = mode_pos.shape
    half = n_dom // 2
    total = n_bead * beads
    group = 2 if beads % 4 == 0 else 1
    vmem, smem = pl.BlockSpec(memory_space=pltpu.VMEM), pl.BlockSpec(memory_space=pltpu.SMEM)
    shape = jax.ShapeDtypeStruct(mode_pos.shape, jnp.float32)
    return pl.pallas_call(
        functools.partial(kernel, n_bead, n_dom),
        out_shape=(shape, shape),
        in_specs=[smem, smem, vmem, vmem, vmem],
        out_specs=(vmem, vmem),
        scratch_shapes=[
            pltpu.VMEM((n_bead, beads, 8, count), jnp.float32),
            pltpu.VMEM((half + 1, beads, 8, count), jnp.float32),
            pltpu.VMEM((beads, 8, count), jnp.float32),
            pltpu.VMEM((beads, 8, count), jnp.float32),
            pltpu.VMEM((beads, 48, count), jnp.bfloat16),
            pltpu.VMEM((beads, 32, count), jnp.bfloat16),
            pltpu.VMEM((beads, 32, count), jnp.float32),
            pltpu.VMEM((half + 1, beads, 8, count), jnp.float32),
            pltpu.VMEM((half + 1, beads, 8, count), jnp.float32),
            pltpu.VMEM((group, count, count), jnp.float32),
            pltpu.VMEM((group, count, 2 * count), jnp.bfloat16),
            pltpu.VMEM((beads, count, 48), jnp.bfloat16),
            pltpu.VMEM((beads, 32, count), jnp.bfloat16),
            pltpu.VMEM((beads, 32, count), jnp.float32),
            pltpu.SemaphoreType.DMA((n_bead,)),
            pltpu.SemaphoreType.DMA((n_bead,)),
            pltpu.SemaphoreType.DMA((half + 1,)),
            pltpu.SemaphoreType.DMA((half + 1,)),
            pltpu.SemaphoreType.DMA((half + 1,)),
            pltpu.SemaphoreType.DMA((half + 1,)),
        ],
        compiler_params=pltpu.CompilerParams(
            collective_id=0, has_side_effects=True, vmem_limit_bytes=48 * 1024 * 1024
        ),
    )(mode_table(total), step_table(total), mode_pos, mode_vel, charges)


def solution(mesh):
    placed = (P("bead", None, "dom"), P("bead", None, "dom"), P("dom"))
    return jax.shard_map(
        local,
        mesh=mesh,
        in_specs=placed,
        out_specs=(P("bead", None, "dom"), P("bead", None, "dom")),
        check_vma=False,
    )
```
